128 devices in a mesh: pipe: 2 (over core), fsdp: 16 (over z, y), tp: 4 (over x).
Axes of the slice: x: 4, y: 4, z: 4, core: 2. Of those that a mesh axis runs over, the one named last changes fastest.
Arguments:
- boundary: bfloat16 [2, 2, 12608, 768], P('pipe', None, ('fsdp', 'tp')), may hold values from -6 to 6
- loads: int32 [2, 16], P(None, 'fsdp'), may hold values from 1 to 4, as said below
- norm_gains: bfloat16 [2, 2, 768], P('pipe', None, ('fsdp', 'tp')), may hold values from 0.5 to 1.5
- row_biases: bfloat16 [2, 4, 768], P('pipe', None, ('fsdp', 'tp')), may hold values from -1.796875 to 1.796875
- w_qkv: bfloat16 [2, 768, 3, 12, 64], P('pipe', 'fsdp', None, 'tp'), may hold values from -0.21875 to 0.21875
- qv_bias: bfloat16 [2, 2, 12, 64], P('pipe', None, 'tp', 'fsdp'), may hold values from -1.796875 to 1.796875
- w_out: bfloat16 [2, 12, 64, 768], P('pipe', 'tp', None, 'fsdp'), may hold values from -0.875 to 0.875
- w_up: bfloat16 [2, 768, 3072], P('pipe', None, ('fsdp', 'tp')), may hold values from -0.21875 to 0.21875
- up_bias: bfloat16 [2, 3072], P('pipe', ('fsdp', 'tp')), may hold values from -1.796875 to 1.796875
- w_down: bfloat16 [2, 3072, 768], P('pipe', ('fsdp', 'tp')), may hold values from -0.109375 to 0.109375
Outputs:
- ends: bfloat16 [2, 2, 12608, 768], P('pipe', None, ('fsdp', 'tp'))
- grad_gains: float32 [2, 2, 768], P('pipe', None, ('fsdp', 'tp'))
- grad_biases: float32 [2, 4, 768], P('pipe', None, ('fsdp', 'tp'))
- grad_qkv: float32 [2, 768, 3, 12, 64], P('pipe', 'fsdp', None, 'tp')
- grad_qv_bias: float32 [2, 2, 12, 64], P('pipe', None, 'tp', 'fsdp')
- grad_out: float32 [2, 12, 64, 768], P('pipe', 'tp', None, 'fsdp')
- grad_up: float32 [2, 768, 3072], P('pipe', None, ('fsdp', 'tp'))
- grad_up_bias: float32 [2, 3072], P('pipe', ('fsdp', 'tp'))
- grad_down: float32 [2, 3072, 768], P('pipe', ('fsdp', 'tp'))
The draws below stay inside these ranges and needn't reach their ends.
Inputs may be any that keep to these rules, and one draw needn't show every extreme that they name: loads[m, f] is the number of live images of image group f in micro-batch m; its live images are the first slots; in every micro-batch some group has all 4 slots live.
All inputs are finite; a program needn't handle non-finite values.
Results may differ from the reference program's by a relative error of at most 0.024.
Values may be sent and summed in bfloat16 or wider, within the bound.
A program may use at most 128 MiB of HBM per device.

```python
import jax
import jax.numpy as jnp
from jax import lax

D = 768
HEADS = 12
HD = 64
FF = 3072
SEQ = 197
MB = 2
CAP = 4
GROUPS = 16
ROWS = 12608


def draw_loads(key, part):
    first_key, second_key = jax.random.split(jax.random.fold_in(key, 17))
    base = jax.random.randint(first_key, (MB, GROUPS), 1, CAP + 1)
    filled = jax.random.randint(second_key, (MB,), 0, GROUPS)
    chosen = jnp.arange(GROUPS, dtype=jnp.int32)[None, :] == filled[:, None]
    return jnp.where(chosen, CAP, base).astype(jnp.int32)


def steps_of(own_key, shape, cuts, smallest, high):
    factor_of, own = 1.0, jax.random.fold_in(own_key, 6)
    for axis_at, parts in cuts:
        steps = jnp.exp(jax.random.uniform(jax.random.fold_in(own, axis_at), (parts,), jnp.float32, smallest / len(cuts), high / len(cuts)))
        factor_of = factor_of * jnp.repeat(steps, shape[axis_at] // parts).reshape([-1 if axis == axis_at else 1 for axis in range(len(shape))])
    return factor_of


def noise(rng, shape, deviation, most, shards=(), kind=jnp.bfloat16):
    drawn = jax.random.normal(rng, shape, jnp.float32) * deviation
    if len(shards) > 0:
        drawn = steps_of(rng, shape, shards, -0.22, 0.18) * drawn
    return jnp.clip(drawn, min=-most, max=most).astype(kind)


def setup_inputs(seed: int = 0) -> dict:
    arg_keys = jax.random.split(jax.random.key(seed), 11)
    boundary = noise(arg_keys[0], (2, MB, ROWS, D), 1.0, 6.0, ((0, 2), (2, 64)))
    loads = draw_loads(jax.random.fold_in(arg_keys[10], 71), 0)
    norm_gains = jnp.clip(1.0 + 0.1 * jax.random.normal(arg_keys[2], (2, 2, D), jnp.float32), 0.5, 1.5).astype(jnp.bfloat16)
    row_biases = noise(arg_keys[3], (2, 4, D), 0.3, 1.796875, ((0, 2), (2, 64)))
    w_qkv = noise(arg_keys[4], (2, D, 3, HEADS, HD), D ** -0.5, 0.21875, ((0, 2), (1, 16), (3, 4)))
    qv_bias = noise(arg_keys[5], (2, 2, HEADS, HD), 0.3, 1.796875, ((0, 2), (2, 4), (3, 16)))
    w_out = noise(arg_keys[6], (2, HEADS, HD, D), (D // 16) ** -0.5, 0.875, ((0, 2), (1, 4), (3, 16)))
    w_up = noise(arg_keys[7], (2, D, FF), D ** -0.5, 0.21875, ((0, 2), (2, 64)))
    up_bias = noise(arg_keys[8], (2, FF), 0.3, 1.796875, ((0, 2), (1, 64)))
    w_down = noise(arg_keys[9], (2, FF, D), FF ** -0.5, 0.109375, ((0, 2), (1, 64)))
    return dict(boundary=boundary, loads=loads, norm_gains=norm_gains, row_biases=row_biases, w_qkv=w_qkv, qv_bias=qv_bias, w_out=w_out, w_up=w_up, up_bias=up_bias, w_down=w_down)


@jax.custom_vjp
def low(v):
    return lax.optimization_barrier(v.astype(jnp.bfloat16)).astype(jnp.float32)

@jax.custom_vjp
def low_back(v):
    return v

def low_keep(v):
    return (low(v), None)

def low_pass(kept, grad):
    return (grad,)

def back_keep(v):
    return (v, None)

def back_low(kept, grad):
    return (low(grad),)
low.defvjp(low_keep, low_pass)
low_back.defvjp(back_keep, back_low)
highest = lax.Precision.HIGHEST
epsilon = 1e-06

def normed(values, gain, shift):
    center = values - lax.optimization_barrier(jnp.mean(values, -1, keepdims=True))
    spread = lax.optimization_barrier(jnp.mean(center * center, -1, keepdims=True))
    return center * lax.rsqrt(spread + epsilon) * gain + shift

def layer(section, inputs):
    gain_rows, bias_rows, in_proj, qv_bias, out_proj, up_proj, up_bias, down_proj = section
    norm_one = low(normed(inputs, gain_rows[0], bias_rows[0]))
    bias_three = jnp.stack([qv_bias[0], jnp.zeros_like(qv_bias[0]), qv_bias[1]], 0)
    qkv = jnp.einsum('csd,dthe->csthe', norm_one, in_proj, precision=highest) + bias_three
    qkv = low(low_back(qkv))
    query_rows = qkv[:, :, 0]
    key_rows = qkv[:, :, 1]
    value_rows = qkv[:, :, 2]
    scale = HD ** (-0.5)
    scores = low_back(jnp.einsum('cqhe,ckhe->chqk', query_rows, key_rows, precision=highest) * scale)
    probs = jax.nn.softmax(scores, axis=-1)
    mixed = jnp.einsum('chqk,ckhe->cqhe', low(probs), value_rows, precision=highest)
    mixed = low(low_back(mixed))
    attn = jnp.einsum('cshe,hed->csd', mixed, out_proj, precision=highest) + bias_rows[1]
    middle = inputs + low_back(attn)
    norm_two = low(normed(middle, gain_rows[1], bias_rows[2]))
    upper = low_back(jnp.einsum('csd,df->csf', norm_two, up_proj, precision=highest) + up_bias)
    activated = low(jax.nn.gelu(upper, approximate=False))
    result = jnp.einsum('csf,fd->csd', activated, down_proj, precision=highest) + bias_rows[3]
    return middle + low_back(result)

def pick_section(params, index):
    return tuple((item[index] for item in params))

def chain(params, inputs, live_mask):
    first_out = layer(pick_section(params, 0), inputs)
    second_in = low(low_back(first_out))
    second_out = layer(pick_section(params, 1), second_in)
    return second_out * live_mask[:, None, None]

def reference(boundary, loads, norm_gains, row_biases, w_qkv, qv_bias, w_out, w_up, up_bias, w_down):
    params = tuple((item.astype(jnp.float32) for item in (norm_gains, row_biases, w_qkv, qv_bias, w_out, w_up, up_bias, w_down)))
    inputs = boundary[0].astype(jnp.float32).reshape(MB * GROUPS, CAP, SEQ, D)
    cotangent = boundary[1].astype(jnp.float32).reshape(MB * GROUPS, CAP, SEQ, D)
    live = (jnp.arange(CAP, dtype=jnp.int32)[None, :] < loads.reshape(-1)[:, None]).astype(jnp.float32)

    def step(totals, item):
        block_in, block_cot, block_live = item

        def run(weights, rows_in):
            return chain(weights, rows_in, block_live)
        result, pull = jax.vjp(run, params, block_in)
        grad_params, grad_in = pull(block_cot)
        totals = jax.tree.map(jnp.add, totals, grad_params)
        return (totals, (result, grad_in))
    zeros = jax.tree.map(jnp.zeros_like, params)
    totals, (results, grads_in) = lax.scan(step, zeros, (inputs, cotangent, live))
    ends = jnp.stack([grads_in.reshape(MB, ROWS, D), results.reshape(MB, ROWS, D)], 0).astype(jnp.bfloat16)
    return (ends, totals[0], totals[1], totals[2], totals[3], totals[4], totals[5], totals[6], totals[7])
```

```python
import types

import jax
import jax.numpy as jnp
from jax import lax
from jax.experimental import pallas as pl
from jax.experimental.pallas import tpu as pltpu
from jax.sharding import PartitionSpec as P

MESH = pl.DeviceIdType.MESH
bf16 = jnp.bfloat16
f32 = jnp.float32


ORDERS = (("x", "y", "z"), ("y", "z", "x"), ("z", "x", "y"))
LAYOUT = (("x", "z", "y"), ("z", "y", "x"), ("z", "y", "x"))


def place():
    f = lax.axis_index("fsdp")
    return {"z": f // 4, "y": lax.rem(f, 4), "x": lax.axis_index("tp")}


def device_at(coords):
    return {"fsdp": coords["z"] * 4 + coords["y"], "tp": coords["x"]}


def moved(coords, axis, by):
    out = dict(coords)
    out[axis] = lax.rem(coords[axis] + by, 4)
    return out


def sibling():
    return {"pipe": 1 - lax.axis_index("pipe")}


def enter(coords):
    barrier = pltpu.get_barrier_semaphore()
    for axis in ("x", "y", "z"):
        for by in (1, 2, 3):
            pl.semaphore_signal(barrier, inc=1, device_id=device_at(moved(coords, axis, by)), device_id_type=MESH)
    pl.semaphore_signal(barrier, inc=1, device_id=sibling(), device_id_type=MESH)
    pl.semaphore_wait(barrier, 10)


def block_of(buf, coords, kind, third, free, axis, value, half):
    index, cols = [], slice(None)
    uncut = half is not None
    for name in LAYOUT[kind]:
        if name in free:
            index.append(pl.ds(half * 2, 2) if uncut else slice(None))
            uncut = False
        else:
            index.append(value if name == axis else coords[name])
    if uncut:
        cols = pl.ds(half * 384, 384)
    return buf.at[(kind, *index, pl.ds(third * 16, 16), cols)]


class Gather:
    def __init__(self, buf, kind, third, coords, send, recv):
        self.buf, self.kind, self.third, self.coords = buf, kind, third, coords
        self.send, self.recv, self.sid = send, recv, kind * 3 + third

    def copy(self, phase, which):
        order = ORDERS[self.third]
        axis = order[phase]
        me = self.coords[axis]
        value = (me, me, lax.rem(me + 3, 4), lax.rem(me + 1, 4))[which]
        ref = block_of(
            self.buf, self.coords, self.kind, self.third, order[:phase], axis, value, (None, None, 0, 1)[which]
        )
        return pltpu.make_async_remote_copy(
            src_ref=ref,
            dst_ref=ref,
            send_sem=self.send.at[self.sid, phase, which],
            recv_sem=self.recv.at[self.sid, phase, which],
            device_id=device_at(moved(self.coords, axis, (1, 3)[which % 2])),
            device_id_type=MESH,
        )

    def step(self, number):
        phase, stage = number // 3, number % 3
        if stage == 0:
            self.copy(phase, 0).start()
            self.copy(phase, 1).start()
        elif stage == 1:
            self.copy(phase, 0).wait_recv()
            self.copy(phase, 2).start()
            self.copy(phase, 1).wait_recv()
            self.copy(phase, 3).start()
        else:
            self.copy(phase, 2).wait_recv()
            self.copy(phase, 3).wait_recv()

    def drain(self):
        for phase in range(3):
            for which in range(4):
                self.copy(phase, which).wait_send()


class Scatter:
    def __init__(self, buf, kind, third, coords, landings, send, recv, out):
        self.buf, self.kind, self.third, self.coords = buf, kind, third, coords
        self.landings, self.send, self.recv, self.sid, self.out = landings, send, recv, kind * 3 + third, out

    def block(self, phase, by, half):
        order = ORDERS[self.third][::-1]
        axis = order[phase]
        value = lax.rem(self.coords[axis] + by, 4)
        return block_of(self.buf, self.coords, self.kind, self.third, order[phase + 1 :], axis, value, half)

    def landing(self, phase, which):
        return self.landings[2 * phase + which // 2].at[self.sid, which % 2]

    def copy(self, phase, which):
        axis = ORDERS[self.third][::-1][phase]
        by = (2, 2, 1, 3)[which]
        return pltpu.make_async_remote_copy(
            src_ref=self.block(phase, by, (0, 1, None, None)[which]),
            dst_ref=self.landing(phase, which),
            send_sem=self.send.at[self.sid, phase, which],
            recv_sem=self.recv.at[self.sid, phase, which],
            device_id=device_at(moved(self.coords, axis, (1, 3)[which % 2])),
            device_id_type=MESH,
        )

    def step(self, number):
        phase, stage = number // 3, number % 3
        if stage == 0:
            self.copy(phase, 0).start()
            self.copy(phase, 1).start()
        elif stage == 1:
            for which, by in ((0, 1), (1, 3)):
                self.copy(phase, which).wait_recv()
                mine = self.block(phase, by, which)
                mine[...] = (mine[...].astype(f32) + self.landing(phase, which)[...].astype(f32)).astype(bf16)
                self.copy(phase, 2 + which).start()
        else:
            self.copy(phase, 2).wait_recv()
            self.copy(phase, 3).wait_recv()
            mine = self.block(phase, 0, None)
            total = (
                mine[...].astype(f32)
                + self.landing(phase, 2)[...].astype(f32)
                + self.landing(phase, 3)[...].astype(f32)
            )
            if phase < 2:
                mine[...] = total.astype(bf16)
            else:
                self.out[pl.ds(self.kind * 48 + self.third * 16, 16), :] = total

    def drain(self):
        for phase in range(3):
            for which in range(4):
                self.copy(phase, which).wait_send()


class AllSum:
    def __init__(self, stages, landings, coords, send, recv):
        self.stages, self.landings, self.coords, self.send, self.recv = stages, landings, coords, send, recv

    def copy(self, phase, which):
        return pltpu.make_async_remote_copy(
            src_ref=self.stages.at[phase],
            dst_ref=self.landings.at[phase, which],
            send_sem=self.send.at[phase, which],
            recv_sem=self.recv.at[phase, which],
            device_id=device_at(moved(self.coords, "xyz"[phase], which + 1)),
            device_id_type=MESH,
        )

    def start(self, phase):
        for which in range(3):
            self.copy(phase, which).start()

    def finish(self, phase):
        for which in range(3):
            self.copy(phase, which).wait_recv()
        self.stages[phase + 1] = (self.stages[phase] + self.landings[phase, 0]) + (
            self.landings[phase, 1] + self.landings[phase, 2]
        )

    def drain(self):
        for phase in range(3):
            for which in range(3):
                self.copy(phase, which).wait_send()


LANDINGS = [
    pltpu.VMEM((9, 2, 2, 4, 16, 768), bf16),
    pltpu.VMEM((9, 2, 4, 4, 16, 768), bf16),
    pltpu.VMEM((9, 2, 2, 16, 768), bf16),
    pltpu.VMEM((9, 2, 4, 16, 768), bf16),
    pltpu.VMEM((9, 2, 16, 384), bf16),
    pltpu.VMEM((9, 2, 16, 768), bf16),
]


SEQ, IMG, ROWS = 197, 208, 416
CHUNK = 32
EPS = 1e-6


def nn(a, b):
    return jnp.dot(a, b, preferred_element_type=f32)


def nt(a, b):
    return lax.dot_general(a, b, (((1,), (1,)), ((), ())), preferred_element_type=f32)


def tn(a, b):
    return lax.dot_general(a, b, (((0,), (0,)), ((), ())), preferred_element_type=f32)


def normed(v):
    center = v - jnp.mean(v, -1, keepdims=True)
    inv = lax.rsqrt(jnp.mean(center * center, -1, keepdims=True) + EPS)
    return center * inv, inv


def norm_back(dn, xhat, inv, gain):
    scaled = dn * gain
    return inv * (scaled - jnp.mean(scaled, -1, keepdims=True)
                  - xhat * jnp.mean(scaled * xhat, -1, keepdims=True))


def fold(v):
    return jnp.sum(v.reshape(v.shape[0] // 8, 8, v.shape[1]), axis=0)


def row_loop(body, init=None):
    def step(i, carry):
        return body(pl.ds(pl.multiple_of(i * CHUNK, CHUNK), CHUNK), carry)
    return lax.fori_loop(0, ROWS // CHUNK, step, init)


def square(ref, kind, j, lo=0, hi=768):
    return ref[kind, j, :, :, :, lo:hi].reshape(768, hi - lo)


def forward(r):
    vec = r.vec

    def first_norm(rows, _):
        xhat, _inv = normed(r.x[rows, :].astype(f32))
        r.n1[rows, :] = (xhat * vec[0:1, :] + vec[2:3, :]).astype(bf16)
    row_loop(first_norm)

    low = lax.broadcasted_iota(jnp.int32, (IMG, 128), 1) < 64
    keyed = lax.broadcasted_iota(jnp.int32, (IMG, IMG), 1) < SEQ
    zero = jnp.zeros((IMG, 128), bf16)

    def head_group(t, _):
        r.q[t] = (nn(r.n1[...], square(r.w, 0, t, 0, 640)) + vec[pl.ds(10 + t, 1), 0:640]).astype(bf16)

        def image(i, _):
            rows = pl.ds(pl.multiple_of(i * IMG, IMG), IMG)
            tq, tk, tv, t3, t4 = (r.q[t, rows, k * 128:(k + 1) * 128] for k in range(5))

            def probs(h, qs, ks):
                s = nt(qs, ks) * 0.125
                s = jnp.where(keyed, s, -1e30)
                e = jnp.exp(s - jnp.max(s, -1, keepdims=True))
                p = (e * (1.0 / jnp.sum(e, -1, keepdims=True))).astype(bf16)
                r.p[(t * 2 + i) * 3 + h] = p
                return p
            p0 = probs(0, jnp.where(low, tq, zero), tk)
            p1 = probs(1, jnp.where(low, zero, tq), tk)
            p2 = probs(2, jnp.where(low, t3, zero), t4)
            r.mx[t, rows, 0:128] = jnp.where(low, 0.0, nn(p2, t3)).astype(bf16)
            r.mx[t, rows, 128:256] = jnp.where(low, nn(p0, tv), nn(p1, tv)).astype(bf16)
            return 0
        lax.fori_loop(0, 2, image, 0)
        part = nt(r.mx[t], square(r.w, 0, t, 512, 768))

        @pl.when(t == 0)
        def _():
            r.acc[...] = part

        @pl.when(t > 0)
        def _():
            r.acc[...] += part
        return 0
    lax.fori_loop(0, 4, head_group, 0)

    def second_norm(rows, _):
        h1 = r.x[rows, :].astype(f32) + r.acc[rows, :] + vec[3:4, :]
        r.h1[rows, :] = h1
        xhat, _inv = normed(h1)
        r.n2[rows, :] = (xhat * vec[1:2, :] + vec[4:5, :]).astype(bf16)
        r.acc[rows, :] = h1 + vec[5:6, :]
    row_loop(second_norm)

    def hidden(j, _):
        r.tmp[...] = nt(r.n2[...], square(r.w, 1, j)) + vec[pl.ds(6 + j, 1), :]

        def gelu(rows, _):
            u = r.tmp[rows, :]
            cdf = 0.5 * (1.0 + lax.erf(u * 0.7071067811865476))
            r.act[j, rows, :] = (u * cdf).astype(bf16)
            r.gp[j, rows, :] = (cdf + u * (jnp.exp(-0.5 * u * u) * 0.3989422804014327)).astype(bf16)
        row_loop(gelu)
        r.acc[...] += nn(r.act[j], square(r.w, 2, j))
        return 0
    lax.fori_loop(0, 4, hidden, 0)


def backward_ffn(r):
    vec = r.vec
    dvec = r.dvec

    def hidden(j, _):
        r.tmp[...] = nt(r.gy[...], square(r.w, 2, j))

        def chain(rows, total):
            du = (r.tmp[rows, :] * r.gp[j, rows, :].astype(f32)).astype(bf16)
            r.dx[rows, :] = du
            return total + fold(du.astype(f32))
        total = row_loop(chain, jnp.zeros((8, 768), f32))
        dvec[pl.ds(6 + j, 1), :] = jnp.sum(total, 0, keepdims=True)
        r.g[2, j] = tn(r.act[j], r.gy[...]).astype(bf16).reshape(4, 4, 48, 768)
        r.g[1, j] = tn(r.dx[...], r.n2[...]).astype(bf16).reshape(4, 4, 48, 768)
        part = nn(r.dx[...], square(r.w, 1, j))

        @pl.when(j == 0)
        def _():
            r.acc[...] = part

        @pl.when(j > 0)
        def _():
            r.acc[...] += part
        return 0
    lax.fori_loop(0, 4, hidden, 0)

    def norm_two(rows, sums):
        dn = r.acc[rows, :]
        gy = r.gy[rows, :].astype(f32)
        xhat, inv = normed(r.h1[rows, :])
        dh = gy + norm_back(dn, xhat, inv, vec[1:2, :])
        r.tmp[rows, :] = dh
        gh = dh.astype(bf16)
        r.n2[rows, :] = gh
        return (sums[0] + fold(dn * xhat), sums[1] + fold(dn), sums[2] + fold(gh.astype(f32)), sums[3] + fold(gy))
    zero = jnp.zeros((8, 768), f32)
    sums = row_loop(norm_two, (zero,) * 4)
    for row, total in zip((1, 4, 3, 5), sums):
        dvec[row:row + 1, :] = jnp.sum(total, 0, keepdims=True)


def backward_attention(r):
    vec = r.vec
    dvec = r.dvec
    dqkv, dmixed = r.gp.at[0], r.gp.at[1]
    low = lax.broadcasted_iota(jnp.int32, (IMG, 128), 1) < 64
    zero = jnp.zeros((IMG, 128), bf16)

    def head_group(t, _):
        dmixed[:, 0:256] = nn(r.n2[...], square(r.w, 0, t, 512, 768)).astype(bf16)

        def image(i, _):
            rows = pl.ds(pl.multiple_of(i * IMG, IMG), IMG)
            tq, tk, tv, t3, t4 = (r.q[t, rows, k * 128:(k + 1) * 128] for k in range(5))
            d4 = dmixed[rows, 0:128]
            d5 = dmixed[rows, 128:256]

            def head(h, d_full, d_masked, v, q, k):
                p = r.p[(t * 2 + i) * 3 + h]
                pf = p.astype(f32)
                dv = tn(p, d_full)
                dp = nt(d_masked, v)
                ds = (pf * (dp - jnp.sum(dp * pf, -1, keepdims=True))).astype(bf16)
                return nn(ds, k) * 0.125, tn(ds, q) * 0.125, dv
            dq0, dk0, dv0 = head(0, d5, jnp.where(low, d5, zero), tv, tq, tk)
            dq1, dk1, dv1 = head(1, d5, jnp.where(low, zero, d5), tv, tq, tk)
            dqkv[rows, 0:128] = jnp.where(low, dq0, dq1).astype(bf16)
            dqkv[rows, 128:256] = jnp.where(low, dk0, dk1).astype(bf16)
            dqkv[rows, 256:384] = jnp.where(low, dv0, dv1).astype(bf16)
            dq2, dk2, dv2 = head(2, d4, jnp.where(low, zero, d4), t3, t3, t4)
            dqkv[rows, 384:512] = jnp.where(low, dq2, dv2).astype(bf16)
            dqkv[rows, 512:640] = jnp.where(low, dk2, 0.0).astype(bf16)
            return 0
        lax.fori_loop(0, 2, image, 0)
        dvec[pl.ds(10 + t, 1), 0:640] = jnp.sum(dqkv[:, 0:640].astype(f32), 0, keepdims=True)
        ga = tn(r.n1[...], dqkv[:, 0:640])
        go = tn(r.n2[...], r.mx[t])
        r.g[0, t, :, :, :, 0:512] = ga[:, 0:512].astype(bf16).reshape(4, 4, 48, 512)
        r.g[0, t, :, :, :, 512:640] = (ga[:, 512:640] + go[:, 0:128]).astype(bf16).reshape(4, 4, 48, 128)
        r.g[0, t, :, :, :, 640:768] = go[:, 128:256].astype(bf16).reshape(4, 4, 48, 128)
        part = nt(dqkv[:, 0:640], square(r.w, 0, t, 0, 640))

        @pl.when(t == 0)
        def _():
            r.acc[...] = part

        @pl.when(t > 0)
        def _():
            r.acc[...] += part
        return 0
    lax.fori_loop(0, 4, head_group, 0)

    def norm_one(rows, sums):
        dn = r.acc[rows, :]
        xhat, inv = normed(r.x[rows, :].astype(f32))
        dx = r.tmp[rows, :] + norm_back(dn, xhat, inv, vec[0:1, :])
        r.dx[rows, :] = dx.astype(bf16)
        return (sums[0] + fold(dn * xhat), sums[1] + fold(dn))
    zero = jnp.zeros((8, 768), f32)
    sums = row_loop(norm_one, (zero,) * 2)
    for row, total in zip((0, 2), sums):
        dvec[row:row + 1, :] = jnp.sum(total, 0, keepdims=True)


SLOTS = (3, 4, 4, 4, 48, 768)
BODY_SCRATCH = dict(
    x=pltpu.VMEM((ROWS, 768), bf16), n1=pltpu.VMEM((ROWS, 768), bf16), q=pltpu.VMEM((4, ROWS, 640), bf16),
    p=pltpu.VMEM((24, IMG, IMG), bf16), mx=pltpu.VMEM((4, ROWS, 256), bf16), acc=pltpu.VMEM((ROWS, 768), f32),
    h1=pltpu.VMEM((ROWS, 768), f32), n2=pltpu.VMEM((ROWS, 768), bf16), act=pltpu.VMEM((4, ROWS, 768), bf16),
    gp=pltpu.VMEM((4, ROWS, 768), bf16), tmp=pltpu.VMEM((ROWS, 768), f32), gy=pltpu.VMEM((ROWS, 768), bf16),

    dx=pltpu.VMEM((ROWS, 768), bf16),
    vec=pltpu.VMEM((16, 768), f32), dvec=pltpu.VMEM((16, 768), f32),
    w=pltpu.VMEM(SLOTS, bf16), g=pltpu.VMEM(SLOTS, bf16),
)


NAMES = list(BODY_SCRATCH)


def layer_kernel(w_hbm, rows_hbm, vec_hbm, end_hbm, grad_hbm, dvec_hbm, *scratch):
    r = types.SimpleNamespace(**dict(zip(NAMES, scratch)))
    rest = scratch[len(NAMES) :]
    landings, out = rest[:6], r.acc
    stages, sum_landings, ag_send, ag_recv, rs_send, rs_recv, sum_send, sum_recv, link, local = rest[6:]
    coords = place()
    first = lax.axis_index("pipe") == 0
    second = lax.axis_index("pipe") == 1
    enter(coords)

    own = [
        pltpu.make_async_copy(
            w_hbm.at[kind], r.w.at[(kind, *(coords[name] for name in LAYOUT[kind]))], local.at[kind]
        )
        for kind in range(3)
    ]
    for copy in own:
        copy.start()
    vec_in = pltpu.make_async_copy(vec_hbm, stages.at[0, 0], local.at[3])
    vec_in.start()

    @pl.when(first)
    def _():
        copy = pltpu.make_async_copy(rows_hbm, r.x, local.at[4])
        copy.start()
        copy.wait()

    @pl.when(second)
    def _():
        copy = pltpu.make_async_copy(rows_hbm, r.gy, local.at[4])
        copy.start()
        copy.wait()

    for copy in own:
        copy.wait()
    vec_in.wait()

    gathers = [Gather(r.w, kind, third, coords, ag_send, ag_recv) for kind in range(3) for third in range(3)]
    sums = [
        AllSum(stages.at[k], sum_landings.at[k], coords, sum_send.at[k], sum_recv.at[k]) for k in range(2)
    ]
    for number in range(9):
        for gather in gathers:
            gather.step(number)
        if number % 3 == 0:
            sums[0].start(number // 3)
        elif number % 3 == 1:
            sums[0].finish(number // 3)
    r.vec[...] = stages[0, 3]
    r.dvec[...] = jnp.zeros_like(r.dvec)
    for gather in gathers:
        gather.drain()
    sums[0].drain()

    up = pltpu.make_async_remote_copy(
        src_ref=r.dx, dst_ref=r.x, send_sem=link.at[0], recv_sem=link.at[1], device_id=sibling(), device_id_type=MESH
    )
    down = pltpu.make_async_remote_copy(
        src_ref=r.dx, dst_ref=r.gy, send_sem=link.at[2], recv_sem=link.at[3], device_id=sibling(), device_id_type=MESH
    )
    end = pltpu.make_async_copy(r.dx, end_hbm, local.at[5])

    @pl.when(second)
    def _():
        up.wait_recv()

    forward(r)
    r.dx[...] = r.acc[...].astype(bf16)

    @pl.when(first)
    def _():
        up.start()
        up.wait_send()
        down.wait_recv()

    @pl.when(second)
    def _():
        end.start()
        end.wait()

    backward_ffn(r)
    scatters = [
        Scatter(r.g, kind, third, coords, landings, rs_send, rs_recv, out) for kind in range(3) for third in range(3)
    ]
    for scatter in scatters[3:]:
        scatter.step(0)
    backward_attention(r)

    @pl.when(first)
    def _():
        end.start()
        end.wait()

    @pl.when(second)
    def _():
        down.start()
        down.wait_send()

    stages[1, 0] = r.dvec[...]
    for scatter in scatters[:3]:
        scatter.step(0)
    for number in range(9):
        for scatter in scatters:
            if number:
                scatter.step(number)
        if number % 3 == 0:
            sums[1].start(number // 3)
        elif number % 3 == 1:
            sums[1].finish(number // 3)
    for scatter in scatters:
        scatter.drain()
    sums[1].drain()
    copies = [
        pltpu.make_async_copy(out.at[pl.ds(0, 144)], grad_hbm, local.at[0]),
        pltpu.make_async_copy(stages.at[1, 3], dvec_hbm, local.at[1]),
    ]
    for copy in copies:
        copy.start()
    for copy in copies:
        copy.wait()


def units(q, k, v, o):
    order = ((q, 0), (q, 1), (k, 0), (k, 1), (v, 0), (v, 1), (q, 2), (v, 2), (k, 2), (o, 2), (o, 0), (o, 1))
    return jnp.concatenate([a[..., h, :] for a, h in order], -1)


def split_units(joined):
    part = [joined[..., 64 * n : 64 * n + 64] for n in range(joined.shape[-1] // 64)]
    pick = lambda *numbers: jnp.stack([part[n] for n in numbers], -2)
    return pick(0, 1, 6), pick(2, 3, 8), pick(4, 5, 7), (pick(10, 11, 9) if len(part) > 10 else None)


def on_device(
    boundary, loads, norm_gains, row_biases, w_qkv, qv_bias, w_out, w_up, up_bias, w_down
):
    first = lax.axis_index("pipe") == 0
    fsdp, tp = lax.axis_index("fsdp"), lax.axis_index("tp")
    chip = fsdp * 4 + tp
    live = (tp < loads[:, 0])[:, None, None]
    rows = jnp.where(first | live, boundary[0], 0)
    rows = jnp.pad(rows, ((0, 0), (0, IMG - SEQ), (0, 0))).reshape(ROWS, 768)

    wq = w_qkv[0]
    wo = w_out[0].transpose(2, 0, 1)
    weights = jnp.stack([units(wq[:, 0], wq[:, 1], wq[:, 2], wo), w_up[0].T, w_down[0]], 0)

    lanes = jnp.arange(768, dtype=jnp.int32)
    small = jnp.concatenate([norm_gains[0], row_biases[0]], 0).astype(f32)
    small = jnp.where(lanes // 12 == chip, jnp.tile(small, (1, 64)), 0.0)
    hidden = jnp.arange(3072, dtype=jnp.int32)
    hidden = jnp.where(hidden // 48 == chip, jnp.tile(up_bias[0].astype(f32), 64), 0.0).reshape(4, 768)
    heads = jnp.where(
        jnp.arange(64, dtype=jnp.int32) // 4 == fsdp, jnp.tile(qv_bias[0].astype(f32), (1, 1, 16)), 0.0
    )
    none = jnp.zeros_like(heads[0])
    heads = units(heads[0], none, heads[1], none)
    heads = jnp.where(jnp.arange(4, dtype=jnp.int32)[:, None] == tp, heads[None], 0.0)
    vec = jnp.concatenate([small, hidden, heads, jnp.zeros((2, 768), f32)], 0)

    anywhere = pl.BlockSpec(memory_space=pl.ANY)
    dma = pltpu.SemaphoreType.DMA
    end, grads, dvec = pl.pallas_call(
        layer_kernel,
        out_shape=(
            jax.ShapeDtypeStruct((ROWS, 768), bf16),
            jax.ShapeDtypeStruct((144, 768), f32),
            jax.ShapeDtypeStruct((16, 768), f32),
        ),
        in_specs=[anywhere] * 3,
        out_specs=(anywhere,) * 3,
        scratch_shapes=[
            *BODY_SCRATCH.values(),
            *LANDINGS,
            pltpu.VMEM((2, 4, 16, 768), f32),
            pltpu.VMEM((2, 3, 3, 16, 768), f32),
            dma((9, 3, 4)),
            dma((9, 3, 4)),
            dma((9, 3, 4)),
            dma((9, 3, 4)),
            dma((2, 3, 3)),
            dma((2, 3, 3)),
            dma((4,)),
            dma((6,)),
        ],
        compiler_params=pltpu.CompilerParams(
            collective_id=0, has_side_effects=True, vmem_limit_bytes=63 * 2**20
        ),
    )(weights, rows, vec)

    end = end.reshape(2, IMG, 768)[:, :SEQ]
    ends = jnp.where(first | live, end, 0)[None]
    gq, gk, gv, go = split_units(grads[:48])
    mine = lax.dynamic_slice(dvec, (0, chip * 12), (6, 12))
    up_row = lax.dynamic_slice(dvec[6:10].reshape(3072), (chip * 48,), (48,))
    head_row = lax.dynamic_slice(dvec, (10 + tp, 0), (1, 640))[0]
    hq, _, hv, _ = split_units(head_row)
    head_grads = lax.dynamic_slice(jnp.stack([hq, hv], 0), (0, 0, fsdp * 4), (2, 3, 4))
    return (
        ends,
        mine[:2][None],
        mine[2:][None],
        jnp.stack([gq, gk, gv], 1)[None],
        head_grads[None],
        go.transpose(1, 2, 0)[None],
        grads[48:96].T[None],
        up_row[None],
        grads[96:][None],
    )


def solution(mesh):
    placed = (
        P("pipe", None, ("fsdp", "tp"), None),
        P(None, "fsdp"),
        P("pipe", None, ("fsdp", "tp")),
        P("pipe", None, ("fsdp", "tp")),
        P("pipe", "fsdp", None, "tp", None),
        P("pipe", None, "tp", "fsdp"),
        P("pipe", "tp", None, "fsdp"),
        P("pipe", None, ("fsdp", "tp")),
        P("pipe", ("fsdp", "tp")),
        P("pipe", ("fsdp", "tp"), None),
    )
    return jax.shard_map(
        on_device,
        mesh=mesh,
        in_specs=placed,
        out_specs=(placed[0], *placed[2:]),
        check_vma=False,
    )
```

```python
import types

import jax
import jax.numpy as jnp
from jax import lax
from jax.experimental import pallas as pl
from jax.experimental.pallas import tpu as pltpu
from jax.sharding import PartitionSpec as P

MESH = pl.DeviceIdType.MESH
bf16 = jnp.bfloat16
f32 = jnp.float32


ORDERS = (("x", "y", "z"), ("y", "z", "x"), ("z", "x", "y"))
LAYOUT = (("x", "z", "y"), ("z", "y", "x"), ("z", "y", "x"))


def place():
    f = lax.axis_index("fsdp")
    return {"z": f // 4, "y": lax.rem(f, 4), "x": lax.axis_index("tp")}


def device_at(coords):
    return {"fsdp": coords["z"] * 4 + coords["y"], "tp": coords["x"]}


def moved(coords, axis, by):
    out = dict(coords)
    out[axis] = lax.rem(coords[axis] + by, 4)
    return out


def sibling():
    return {"pipe": 1 - lax.axis_index("pipe")}


def enter(coords):
    barrier = pltpu.get_barrier_semaphore()
    for axis in ("x", "y", "z"):
        for by in (1, 2, 3):
            pl.semaphore_signal(barrier, inc=1, device_id=device_at(moved(coords, axis, by)), device_id_type=MESH)
    pl.semaphore_signal(barrier, inc=1, device_id=sibling(), device_id_type=MESH)
    pl.semaphore_wait(barrier, 10)


def block_of(buf, coords, kind, third, free, axis, value, half):
    index, cols = [], slice(None)
    uncut = half is not None
    for name in LAYOUT[kind]:
        if name in free:
            index.append(pl.ds(half * 2, 2) if uncut else slice(None))
            uncut = False
        else:
            index.append(value if name == axis else coords[name])
    if uncut:
        cols = pl.ds(half * 384, 384)
    return buf.at[(kind, *index, pl.ds(third * 16, 16), cols)]


class Gather:
    def __init__(self, buf, kind, third, coords, send, recv):
        self.buf, self.kind, self.third, self.coords = buf, kind, third, coords
        self.send, self.recv, self.sid = send, recv, kind * 3 + third

    def copy(self, phase, which):
        order = ORDERS[self.third]
        axis = order[phase]
        me = self.coords[axis]
        value = (me, me, lax.rem(me + 3, 4), lax.rem(me + 1, 4))[which]
        ref = block_of(
            self.buf, self.coords, self.kind, self.third, order[:phase], axis, value, (None, None, 0, 1)[which]
        )
        return pltpu.make_async_remote_copy(
            src_ref=ref,
            dst_ref=ref,
            send_sem=self.send.at[self.sid, phase, which],
            recv_sem=self.recv.at[self.sid, phase, which],
            device_id=device_at(moved(self.coords, axis, (1, 3)[which % 2])),
            device_id_type=MESH,
        )

    def step(self, number):
        phase, stage = number // 3, number % 3
        if stage == 0:
            self.copy(phase, 0).start()
            self.copy(phase, 1).start()
        elif stage == 1:
            self.copy(phase, 0).wait_recv()
            self.copy(phase, 2).start()
            self.copy(phase, 1).wait_recv()
            self.copy(phase, 3).start()
        else:
            self.copy(phase, 2).wait_recv()
            self.copy(phase, 3).wait_recv()

    def drain(self):
        for phase in range(3):
            for which in range(4):
                self.copy(phase, which).wait_send()


class Scatter:
    def __init__(self, buf, kind, third, coords, landings, send, recv, out):
        self.buf, self.kind, self.third, self.coords = buf, kind, third, coords
        self.landings, self.send, self.recv, self.sid, self.out = landings, send, recv, kind * 3 + third, out

    def block(self, phase, by, half):
        order = ORDERS[self.third][::-1]
        axis = order[phase]
        value = lax.rem(self.coords[axis] + by, 4)
        return block_of(self.buf, self.coords, self.kind, self.third, order[phase + 1 :], axis, value, half)

    def landing(self, phase, which):
        return self.landings[2 * phase + which // 2].at[self.sid, which % 2]

    def copy(self, phase, which):
        axis = ORDERS[self.third][::-1][phase]
        by = (2, 2, 1, 3)[which]
        return pltpu.make_async_remote_copy(
            src_ref=self.block(phase, by, (0, 1, None, None)[which]),
            dst_ref=self.landing(phase, which),
            send_sem=self.send.at[self.sid, phase, which],
            recv_sem=self.recv.at[self.sid, phase, which],
            device_id=device_at(moved(self.coords, axis, (1, 3)[which % 2])),
            device_id_type=MESH,
        )

    def step(self, number):
        phase, stage = number // 3, number % 3
        if stage == 0:
            self.copy(phase, 0).start()
            self.copy(phase, 1).start()
        elif stage == 1:
            for which, by in ((0, 1), (1, 3)):
                self.copy(phase, which).wait_recv()
                mine = self.block(phase, by, which)
                mine[...] = (mine[...].astype(f32) + self.landing(phase, which)[...].astype(f32)).astype(bf16)
                self.copy(phase, 2 + which).start()
        else:
            self.copy(phase, 2).wait_recv()
            self.copy(phase, 3).wait_recv()
            mine = self.block(phase, 0, None)
            total = (
                mine[...].astype(f32)
                + self.landing(phase, 2)[...].astype(f32)
                + self.landing(phase, 3)[...].astype(f32)
            )
            if phase < 2:
                mine[...] = total.astype(bf16)
            else:
                self.out[pl.ds(self.kind * 48 + self.third * 16, 16), :] = total

    def drain(self):
        for phase in range(3):
            for which in range(4):
                self.copy(phase, which).wait_send()


class AllSum:
    def __init__(self, stages, landings, coords, send, recv):
        self.stages, self.landings, self.coords, self.send, self.recv = stages, landings, coords, send, recv

    def copy(self, phase, which):
        return pltpu.make_async_remote_copy(
            src_ref=self.stages.at[phase],
            dst_ref=self.landings.at[phase, which],
            send_sem=self.send.at[phase, which],
            recv_sem=self.recv.at[phase, which],
            device_id=device_at(moved(self.coords, "xyz"[phase], which + 1)),
            device_id_type=MESH,
        )

    def start(self, phase):
        for which in range(3):
            self.copy(phase, which).start()

    def finish(self, phase):
        for which in range(3):
            self.copy(phase, which).wait_recv()
        total = self.stages[phase].astype(f32)
        for which in range(3):
            total = total + self.landings[phase, which].astype(f32)
        self.stages[phase + 1] = total.astype(self.stages.dtype)

    def drain(self):
        for phase in range(3):
            for which in range(3):
                self.copy(phase, which).wait_send()


LANDINGS = [
    pltpu.VMEM((9, 2, 2, 4, 16, 768), bf16),
    pltpu.VMEM((9, 2, 4, 4, 16, 768), bf16),
    pltpu.VMEM((9, 2, 2, 16, 768), bf16),
    pltpu.VMEM((9, 2, 4, 16, 768), bf16),
    pltpu.VMEM((9, 2, 16, 384), bf16),
    pltpu.VMEM((9, 2, 16, 768), bf16),
]


SEQ, IMG, ROWS = 197, 208, 416
CHUNK = 32
UNROLL = 13
EPS = 1e-6


def nn(a, b):
    return jnp.dot(a, b, preferred_element_type=f32)


def nt(a, b):
    return lax.dot_general(a, b, (((1,), (1,)), ((), ())), preferred_element_type=f32)


def tn(a, b):
    return lax.dot_general(a, b, (((0,), (0,)), ((), ())), preferred_element_type=f32)


def normed(v):
    center = v - jnp.mean(v, -1, keepdims=True)
    inv = lax.rsqrt(jnp.mean(center * center, -1, keepdims=True) + EPS)
    return center * inv, inv


def norm_back(dn, xhat, inv, gain):
    scaled = dn * gain
    return inv * (scaled - jnp.mean(scaled, -1, keepdims=True)
                  - xhat * jnp.mean(scaled * xhat, -1, keepdims=True))


def fold(v):
    return jnp.sum(v.reshape(v.shape[0] // 8, 8, v.shape[1]), axis=0)


def row_loop(body, init=None):
    def step(i, carry):
        return body(pl.ds(pl.multiple_of(i * CHUNK, CHUNK), CHUNK), carry)
    return lax.fori_loop(0, ROWS // CHUNK, step, init, unroll=UNROLL)


def square(ref, kind, j, lo=0, hi=768):
    return ref[kind, j, :, :, :, lo:hi].reshape(768, hi - lo)


def forward_attention(r, hook=None):
    vec = r.vec

    def first_norm(rows, _):
        xhat, _inv = normed(r.x[rows, :].astype(f32))
        r.n1[rows, :] = (xhat * vec[8:9, :] + vec[9:10, :]).astype(bf16)
    row_loop(first_norm)

    low = lax.broadcasted_iota(jnp.int32, (IMG, 128), 1) < 64
    keyed = lax.broadcasted_iota(jnp.int32, (IMG, IMG), 0) < SEQ
    zero = jnp.zeros((IMG, 128), bf16)

    def head_group(t, _):
        r.q[t] = (nn(r.n1[...], square(r.w, 0, t, 0, 640)) + vec[pl.ds(10 + t, 1), 0:640]).astype(bf16)

        def image(i):
            rows = slice(i * IMG, (i + 1) * IMG)
            tq, tk, tv, t3, t4 = (r.q[t, rows, k * 128:(k + 1) * 128] for k in range(5))

            def probs(h, qs, ks):
                s = jnp.where(keyed, nt(ks, qs) * 0.125, -1e30)
                e = jnp.exp(s - jnp.max(s, 0, keepdims=True))
                p = (e * (1.0 / jnp.sum(e, 0, keepdims=True))).astype(bf16)
                r.p[(t * 2 + i) * 3 + h] = p
                return p
            p0 = probs(0, jnp.where(low, tq, zero), tk)
            p1 = probs(1, jnp.where(low, zero, tq), tk)
            p2 = probs(2, jnp.where(low, t3, zero), t4)
            tvt = tv.T
            o01 = jnp.concatenate([nn(tvt[0:64], p0), nn(tvt[64:128], p1)], 0).astype(bf16)
            o2 = jnp.concatenate([jnp.zeros((64, IMG), bf16), nn(t3.T[64:128], p2).astype(bf16)], 0)
            r.mx[t, rows, 0:128] = o2.T
            r.mx[t, rows, 128:256] = o01.T
        image(0)
        image(1)
        part = nt(r.mx[t], square(r.w, 0, t, 512, 768))

        @pl.when(t == 0)
        def _():
            r.acc[...] = part

        @pl.when(t > 0)
        def _():
            r.acc[...] += part
        if hook is not None:
            hook(t)
        return 0
    lax.fori_loop(0, 4, head_group, 0)


def forward_ffn(r):
    vec = r.vec

    def second_norm(rows, _):
        h1 = r.x[rows, :].astype(f32) + r.acc[rows, :] + vec[1:2, :]
        r.h1[rows, :] = h1
        xhat, _inv = normed(h1)
        r.n2[rows, :] = (xhat * vec[0:1, :] + vec[2:3, :]).astype(bf16)
        r.acc[rows, :] = h1 + vec[3:4, :]
    row_loop(second_norm)

    def hidden(j, _):
        up = square(r.w, 1, j)
        for c in range(3):
            cols = slice(c * 256, (c + 1) * 256)
            u = nt(r.n2[...], up[cols]) + vec[pl.ds(4 + j, 1), cols]
            cdf = 0.5 * (1.0 + lax.erf(u * 0.7071067811865476))
            r.act[j, :, cols] = (u * cdf).astype(bf16)
            r.gp[j, :, cols] = (cdf + u * (jnp.exp(-0.5 * u * u) * 0.3989422804014327)).astype(bf16)
        r.acc[...] += nn(r.act[j], square(r.w, 2, j))
        return 0
    lax.fori_loop(0, 4, hidden, 0)


def backward_ffn(r, hook=None):
    vec = r.vec
    dvec = r.dvec

    def hidden(j, _):
        down = square(r.w, 2, j)
        for c in range(3):
            cols = slice(c * 256, (c + 1) * 256)
            du = (nt(r.gy[...], down[cols]) * r.gp[j, :, cols].astype(f32)).astype(bf16)
            r.gp[j, :, cols] = du
            dvec[pl.ds(4 + j, 1), cols] = jnp.sum(du.astype(f32), 0, keepdims=True)
        part = nn(r.gp[j], square(r.w, 1, j))

        @pl.when(j == 0)
        def _():
            r.acc[...] = part

        @pl.when(j > 0)
        def _():
            r.acc[...] += part
        if hook is not None:
            hook(j)
        return 0
    lax.fori_loop(0, 4, hidden, 0)

    def norm_two(rows, sums):
        dn = r.acc[rows, :]
        gy = r.gy[rows, :].astype(f32)
        xhat, inv = normed(r.h1[rows, :])
        dh = gy + norm_back(dn, xhat, inv, vec[0:1, :])
        r.h1[rows, :] = dh
        gh = dh.astype(bf16)
        r.gh[rows, :] = gh
        return (sums[0] + fold(dn * xhat), sums[1] + fold(dn), sums[2] + fold(gh.astype(f32)), sums[3] + fold(gy))
    zero = jnp.zeros((8, 768), f32)
    sums = row_loop(norm_two, (zero,) * 4)
    for row, total in zip((0, 2, 1, 3), sums):
        dvec[row:row + 1, :] = jnp.sum(total, 0, keepdims=True)


def grads_down(r):
    def hidden(j, _):
        r.g[2, j] = tn(r.act[j], r.gy[...]).astype(bf16).reshape(4, 4, 48, 768)
        return 0
    lax.fori_loop(0, 4, hidden, 0)


def grads_up(r):
    def hidden(j, _):
        r.g[1, j] = tn(r.gp[j], r.n2[...]).astype(bf16).reshape(4, 4, 48, 768)
        return 0
    lax.fori_loop(0, 4, hidden, 0)


def backward_attention(r, hook=None):
    dvec = r.dvec
    low = lax.broadcasted_iota(jnp.int32, (IMG, 128), 1) < 64
    zero = jnp.zeros((IMG, 128), bf16)

    def head_group(t, _):
        r.dm[...] = nn(r.gh[...], square(r.w, 0, t, 512, 768)).astype(bf16)

        def image(i):
            rows = slice(i * IMG, (i + 1) * IMG)
            tq, tk, tv, t3, t4 = (r.q[t, rows, k * 128:(k + 1) * 128] for k in range(5))
            d4 = r.dm[rows, 0:128]
            d5 = r.dm[rows, 128:256]

            def head(h, d_full, d_masked, v, q, kt):
                p = r.p[(t * 2 + i) * 3 + h]
                pf = p.astype(f32)
                dv = nn(p, d_full)
                dp = nt(v, d_masked)
                ds = (pf * (dp - jnp.sum(dp * pf, 0, keepdims=True))).astype(bf16)
                return nn(kt, ds), nn(ds, q) * 0.125, dv
            tkt = tk.T
            dq0, dk0, dv0 = head(0, d5, jnp.where(low, d5, zero), tv, tq, tkt[0:64])
            dq1, dk1, dv1 = head(1, d5, jnp.where(low, zero, d5), tv, tq, tkt[64:128])
            dq2, dk2, dv2 = head(2, d4, jnp.where(low, zero, d4), t3, t3, t4.T[0:64])
            r.q[t, rows, 0:128] = (jnp.concatenate([dq0, dq1], 0) * 0.125).astype(bf16).T
            r.q[t, rows, 128:256] = jnp.where(low, dk0, dk1).astype(bf16)
            r.q[t, rows, 256:384] = jnp.where(low, dv0, dv1).astype(bf16)
            dq2 = jnp.concatenate([(dq2 * 0.125).astype(bf16), jnp.zeros((64, IMG), bf16)], 0).T
            r.q[t, rows, 384:512] = jnp.where(low, dq2, dv2.astype(bf16))
            r.q[t, rows, 512:640] = jnp.where(low, dk2, 0.0).astype(bf16)
        image(0)
        image(1)
        dvec[pl.ds(10 + t, 1), 0:640] = jnp.sum(r.q[t].astype(f32), 0, keepdims=True)
        part = nt(r.q[t], square(r.w, 0, t, 0, 640))

        @pl.when(t == 0)
        def _():
            r.acc[...] = part

        @pl.when(t > 0)
        def _():
            r.acc[...] += part
        if hook is not None:
            hook(t)
        return 0
    lax.fori_loop(0, 4, head_group, 0)


def grads_attention(r):
    def head_group(t, _):
        ga = tn(r.n1[...], r.q[t])
        go = tn(r.gh[...], r.mx[t])
        r.g[0, t, :, :, :, 0:512] = ga[:, 0:512].astype(bf16).reshape(4, 4, 48, 512)
        r.g[0, t, :, :, :, 512:640] = (ga[:, 512:640] + go[:, 0:128]).astype(bf16).reshape(4, 4, 48, 128)
        r.g[0, t, :, :, :, 640:768] = go[:, 128:256].astype(bf16).reshape(4, 4, 48, 128)
        return 0
    lax.fori_loop(0, 4, head_group, 0)


def backward_end(r):
    vec = r.vec
    dvec = r.dvec

    def norm_one(rows, sums):
        dn = r.acc[rows, :]
        xhat, inv = normed(r.x[rows, :].astype(f32))
        dx = r.h1[rows, :] + norm_back(dn, xhat, inv, vec[8:9, :])
        r.dx[rows, :] = dx.astype(bf16)
        return (sums[0] + fold(dn * xhat), sums[1] + fold(dn))
    zero = jnp.zeros((8, 768), f32)
    sums = row_loop(norm_one, (zero,) * 2)
    for row, total in zip((8, 9), sums):
        dvec[row:row + 1, :] = jnp.sum(total, 0, keepdims=True)


SLOTS = (3, 4, 4, 4, 48, 768)
BODY_SCRATCH = dict(
    x=pltpu.VMEM((ROWS, 768), bf16), n1=pltpu.VMEM((ROWS, 768), bf16), q=pltpu.VMEM((4, ROWS, 640), bf16),
    p=pltpu.VMEM((24, IMG, IMG), bf16), mx=pltpu.VMEM((4, ROWS, 256), bf16), acc=pltpu.VMEM((ROWS, 768), f32),
    h1=pltpu.VMEM((ROWS, 768), f32), n2=pltpu.VMEM((ROWS, 768), bf16), act=pltpu.VMEM((4, ROWS, 768), bf16),
    gp=pltpu.VMEM((4, ROWS, 768), bf16), gy=pltpu.VMEM((ROWS, 768), bf16), gh=pltpu.VMEM((ROWS, 768), bf16),
    dm=pltpu.VMEM((ROWS, 256), bf16), dx=pltpu.VMEM((ROWS, 768), bf16),
    vec=pltpu.VMEM((16, 768), f32), dvec=pltpu.VMEM((16, 768), f32),
    w=pltpu.VMEM(SLOTS, bf16), g=pltpu.VMEM(SLOTS, bf16),
)


NAMES = list(BODY_SCRATCH)


def layer_kernel(w_hbm, rows_hbm, vec_hbm, end_hbm, grad_hbm, dvec_hbm, *scratch):
    r = types.SimpleNamespace(**dict(zip(NAMES, scratch)))
    rest = scratch[len(NAMES) :]
    landings, out = rest[:6], r.h1
    stages, sum_landings = rest[6:9], rest[9:12]
    ag_send, ag_recv, rs_send, rs_recv, sum_send, sum_recv, link, local, ready = rest[12:]
    coords = place()
    first = lax.axis_index("pipe") == 0
    second = lax.axis_index("pipe") == 1
    enter(coords)

    own = [
        pltpu.make_async_copy(
            w_hbm.at[kind], r.w.at[(kind, *(coords[name] for name in LAYOUT[kind]))], local.at[kind]
        )
        for kind in range(3)
    ]
    for copy in own:
        copy.start()
    vec_in = pltpu.make_async_copy(vec_hbm, stages[0].at[0], local.at[3])
    vec_in.start()

    @pl.when(first)
    def _():
        copy = pltpu.make_async_copy(rows_hbm, r.x, local.at[4])
        copy.start()
        copy.wait()

    @pl.when(second)
    def _():
        copy = pltpu.make_async_copy(rows_hbm, r.gy, local.at[4])
        copy.start()
        copy.wait()

    for copy in own:
        copy.wait()
    vec_in.wait()

    gathers = [Gather(r.w, kind, third, coords, ag_send, ag_recv) for kind in range(3) for third in range(3)]
    sums = [AllSum(stages[k], sum_landings[k], coords, sum_send.at[k], sum_recv.at[k]) for k in range(3)]

    def each(movers, *numbers):
        for number in numbers:
            for mover in movers:
                mover.step(number)

    early, late = gathers[:3], gathers[3:]
    sums[0].start(0)
    each(early, 0)
    each(late, 0)
    sums[0].finish(0)
    sums[0].start(1)
    each(early, 1)
    each(late, 1)
    each(early, 2, 3)
    sums[0].finish(1)
    sums[0].start(2)
    each(late, 2, 3)
    each(early, 4)
    sums[0].finish(2)
    each(late, 4)
    each(early, 5)

    @pl.when(second)
    def _():
        each(late, 5)
        pl.semaphore_wait(ready, 1)

    each(early, 6)

    @pl.when(first)
    def _():
        each(late, 5)

    each(late, 6)
    each(early, 7, 8)

    @pl.when(first)
    def _():
        pl.semaphore_signal(ready, inc=1, device_id=sibling(), device_id_type=MESH)
        each(late, 7)

    r.vec[...] = stages[0][3].astype(f32)
    r.dvec[...] = jnp.zeros_like(r.dvec)

    up = pltpu.make_async_remote_copy(
        src_ref=r.dx, dst_ref=r.x, send_sem=link.at[0], recv_sem=link.at[1], device_id=sibling(), device_id_type=MESH
    )
    down = pltpu.make_async_remote_copy(
        src_ref=r.dx, dst_ref=r.gy, send_sem=link.at[2], recv_sem=link.at[3], device_id=sibling(), device_id_type=MESH
    )
    end = pltpu.make_async_copy(r.dx, end_hbm, local.at[5])

    @pl.when(second)
    def _():
        each(late, 7)
        up.wait_recv()

    forward_attention(r)
    each(late, 8)
    forward_ffn(r)
    r.dx[...] = r.acc[...].astype(bf16)

    @pl.when(first)
    def _():
        up.start()

    @pl.when(second)
    def _():
        end.start()

    for gather in gathers:
        gather.drain()
    sums[0].drain()

    @pl.when(first)
    def _():
        up.wait_send()
        down.wait_recv()

    scatters = [
        Scatter(r.g, kind, third, coords, landings, rs_send, rs_recv, out) for kind in range(3) for third in range(3)
    ]
    sa, su, sd = scatters[:3], scatters[3:6], scatters[6:]
    grads_down(r)
    each(sd, 0)

    def during_ffn(j):
        @pl.when(j == 2)
        def _():
            each(sd, 1)

    backward_ffn(r, during_ffn)
    stages[1][0] = r.dvec[0:8, :]
    sums[1].start(0)
    grads_up(r)
    each(su, 0)
    def during_attention(t):
        @pl.when(t == 3)
        def _():
            sums[1].finish(0)
            sums[1].start(1)
            each(sd, 2, 3)
            each(su, 1)

    backward_attention(r, during_attention)

    @pl.when(second)
    def _():
        end.wait()

    backward_end(r)

    @pl.when(first)
    def _():
        end.start()

    @pl.when(second)
    def _():
        down.start()

    stages[2][0] = r.dvec[8:16, :]
    sums[2].start(0)
    grads_attention(r)
    sums[2].finish(0)
    sums[2].start(1)
    each(sa, 0)
    sums[1].finish(1)
    sums[1].start(2)
    each(sd, 4)
    each(su, 2, 3)
    sums[2].finish(1)
    sums[2].start(2)
    each(sa, 1)
    each(sd, 5, 6)
    each(su, 4)
    sums[1].finish(2)
    each(sa, 2, 3)
    each(sd, 7)
    each(su, 5, 6)
    sums[2].finish(2)
    each(sa, 4)
    each(sd, 8)
    each(su, 7)
    each(sa, 5, 6)
    each(su, 8)
    each(sa, 7, 8)
    copies = [
        pltpu.make_async_copy(out.at[pl.ds(0, 144)], grad_hbm, local.at[0]),
        pltpu.make_async_copy(stages[1].at[3], dvec_hbm.at[pl.ds(0, 8)], local.at[1]),
        pltpu.make_async_copy(stages[2].at[3], dvec_hbm.at[pl.ds(8, 8)], local.at[2]),
    ]
    for copy in copies:
        copy.start()
    for scatter in scatters:
        scatter.drain()
    for some in sums[1:]:
        some.drain()

    @pl.when(first)
    def _():
        end.wait()

    @pl.when(second)
    def _():
        down.wait_send()

    for copy in copies:
        copy.wait()


def units(q, k, v, o):
    order = ((q, 0), (q, 1), (k, 0), (k, 1), (v, 0), (v, 1), (q, 2), (v, 2), (k, 2), (o, 2), (o, 0), (o, 1))
    return jnp.concatenate([a[..., h, :] for a, h in order], -1)


def split_units(joined):
    part = [joined[..., 64 * n : 64 * n + 64] for n in range(joined.shape[-1] // 64)]
    pick = lambda *numbers: jnp.stack([part[n] for n in numbers], -2)
    return pick(0, 1, 6), pick(2, 3, 8), pick(4, 5, 7), (pick(10, 11, 9) if len(part) > 10 else None)


def on_device(
    boundary, loads, norm_gains, row_biases, w_qkv, qv_bias, w_out, w_up, up_bias, w_down
):
    first = lax.axis_index("pipe") == 0
    fsdp, tp = lax.axis_index("fsdp"), lax.axis_index("tp")
    chip = fsdp * 4 + tp
    live = (tp < loads[:, 0])[:, None, None]
    rows = jnp.where(first | live, boundary[0], 0)
    rows = jnp.pad(rows, ((0, 0), (0, IMG - SEQ), (0, 0))).reshape(ROWS, 768)

    wq = w_qkv[0]
    wo = w_out[0].transpose(2, 0, 1)
    weights = jnp.stack([units(wq[:, 0], wq[:, 1], wq[:, 2], wo), w_up[0].T, w_down[0]], 0)

    lanes = jnp.arange(768, dtype=jnp.int32)
    gains, biases = norm_gains[0], row_biases[0]
    small = jnp.concatenate([gains[1:], biases[1:], gains[:1], biases[:1]], 0)
    small = jnp.where(lanes // 12 == chip, jnp.tile(small, (1, 64)), 0)
    hidden = jnp.arange(3072, dtype=jnp.int32)
    hidden = jnp.where(hidden // 48 == chip, jnp.tile(up_bias[0], 64), 0).reshape(4, 768)
    heads = jnp.where(
        jnp.arange(64, dtype=jnp.int32) // 4 == fsdp, jnp.tile(qv_bias[0], (1, 1, 16)), 0
    )
    none = jnp.zeros_like(heads[0])
    heads = units(heads[0], none, heads[1], none)
    heads = jnp.where(jnp.arange(4, dtype=jnp.int32)[:, None] == tp, heads[None], 0)
    vec = jnp.concatenate([small[:4], hidden, small[4:], heads, jnp.zeros((2, 768), bf16)], 0)

    anywhere = pl.BlockSpec(memory_space=pl.ANY)
    dma = pltpu.SemaphoreType.DMA
    end, grads, dvec = pl.pallas_call(
        layer_kernel,
        out_shape=(
            jax.ShapeDtypeStruct((ROWS, 768), bf16),
            jax.ShapeDtypeStruct((144, 768), f32),
            jax.ShapeDtypeStruct((16, 768), f32),
        ),
        in_specs=[anywhere] * 3,
        out_specs=(anywhere,) * 3,
        scratch_shapes=[
            *BODY_SCRATCH.values(),
            *LANDINGS,
            pltpu.VMEM((4, 16, 768), bf16),
            pltpu.VMEM((4, 8, 768), f32),
            pltpu.VMEM((4, 8, 768), f32),
            pltpu.VMEM((3, 3, 16, 768), bf16),
            pltpu.VMEM((3, 3, 8, 768), f32),
            pltpu.VMEM((3, 3, 8, 768), f32),
            dma((9, 3, 4)),
            dma((9, 3, 4)),
            dma((9, 3, 4)),
            dma((9, 3, 4)),
            dma((3, 3, 3)),
            dma((3, 3, 3)),
            dma((4,)),
            dma((6,)),
            pltpu.SemaphoreType.REGULAR,
        ],
        compiler_params=pltpu.CompilerParams(
            collective_id=0, has_side_effects=True, vmem_limit_bytes=63 * 2**20
        ),
    )(weights, rows, vec)

    end = end.reshape(2, IMG, 768)[:, :SEQ]
    ends = jnp.where(first | live, end, 0)[None]
    gq, gk, gv, go = split_units(grads[:48])
    mine = lax.dynamic_slice(dvec, (0, chip * 12), (10, 12))
    up_row = lax.dynamic_slice(dvec[4:8].reshape(3072), (chip * 48,), (48,))
    head_row = lax.dynamic_slice(dvec, (10 + tp, 0), (1, 640))[0]
    hq, _, hv, _ = split_units(head_row)
    head_grads = lax.dynamic_slice(jnp.stack([hq, hv], 0), (0, 0, fsdp * 4), (2, 3, 4))
    return (
        ends,
        jnp.stack([mine[8], mine[0]], 0)[None],
        jnp.stack([mine[9], mine[1], mine[2], mine[3]], 0)[None],
        jnp.stack([gq, gk, gv], 1)[None],
        head_grads[None],
        go.transpose(1, 2, 0)[None],
        grads[48:96].T[None],
        up_row[None],
        grads[96:][None],
    )


def solution(mesh):
    placed = (
        P("pipe", None, ("fsdp", "tp"), None),
        P(None, "fsdp"),
        P("pipe", None, ("fsdp", "tp")),
        P("pipe", None, ("fsdp", "tp")),
        P("pipe", "fsdp", None, "tp", None),
        P("pipe", None, "tp", "fsdp"),
        P("pipe", "tp", None, "fsdp"),
        P("pipe", None, ("fsdp", "tp")),
        P("pipe", ("fsdp", "tp")),
        P("pipe", ("fsdp", "tp"), None),
    )
    return jax.shard_map(
        on_device,
        mesh=mesh,
        in_specs=placed,
        out_specs=(placed[0], *placed[2:]),
        check_vma=False,
    )
```

```python
import types

import jax
import jax.numpy as jnp
from jax import lax
from jax.experimental import pallas as pl
from jax.experimental.pallas import tpu as pltpu
from jax.sharding import PartitionSpec as P

MESH = pl.DeviceIdType.MESH
bf16 = jnp.bfloat16
f32 = jnp.float32


ORDERS = (("x", "y", "z"), ("y", "z", "x"), ("z", "x", "y"))
LAYOUT = (("x", "z", "y"), ("z", "y", "x"), ("z", "y", "x"))


def place():
    f = lax.axis_index("fsdp")
    return {"z": f // 4, "y": lax.rem(f, 4), "x": lax.axis_index("tp")}


def device_at(coords):
    return {"fsdp": coords["z"] * 4 + coords["y"], "tp": coords["x"]}


def moved(coords, axis, by):
    out = dict(coords)
    out[axis] = lax.rem(coords[axis] + by, 4)
    return out


def sibling():
    return {"pipe": 1 - lax.axis_index("pipe")}


def enter(coords):
    barrier = pltpu.get_barrier_semaphore()
    for axis in ("x", "y", "z"):
        for by in (1, 2, 3):
            pl.semaphore_signal(barrier, inc=1, device_id=device_at(moved(coords, axis, by)), device_id_type=MESH)
    pl.semaphore_signal(barrier, inc=1, device_id=sibling(), device_id_type=MESH)
    pl.semaphore_wait(barrier, 10)


def block_of(buf, coords, kind, third, free, axis, value, half):
    index, cols = [], slice(None)
    uncut = half is not None
    for name in LAYOUT[kind]:
        if name in free:
            index.append(pl.ds(half * 2, 2) if uncut else slice(None))
            uncut = False
        else:
            index.append(value if name == axis else coords[name])
    if uncut:
        cols = pl.ds(half * 384, 384)
    return buf.at[(kind, *index, pl.ds(third * 16, 16), cols)]


class Gather:
    def __init__(self, buf, kind, third, coords, send, recv):
        self.buf, self.kind, self.third, self.coords = buf, kind, third, coords
        self.send, self.recv, self.sid = send, recv, kind * 3 + third

    def copy(self, phase, which):
        order = ORDERS[self.third]
        axis = order[phase]
        me = self.coords[axis]
        if phase == 0:
            value, half, by = me, None, which + 1
        else:
            value = (me, me, lax.rem(me + 3, 4), lax.rem(me + 1, 4))[which]
            half, by = (None, None, 0, 1)[which], (1, 3)[which % 2]
        ref = block_of(self.buf, self.coords, self.kind, self.third, order[:phase], axis, value, half)
        return pltpu.make_async_remote_copy(
            src_ref=ref,
            dst_ref=ref,
            send_sem=self.send.at[self.sid, phase, which],
            recv_sem=self.recv.at[self.sid, phase, which],
            device_id=device_at(moved(self.coords, axis, by)),
            device_id_type=MESH,
        )

    def step(self, number):
        phase, stage = number // 3, number % 3
        if phase == 0:
            for which in range(3):
                if stage == 0:
                    self.copy(0, which).start()
                elif stage == 2:
                    self.copy(0, which).wait_recv()
        elif stage == 0:
            self.copy(phase, 0).start()
            self.copy(phase, 1).start()
        elif stage == 1:
            self.copy(phase, 0).wait_recv()
            self.copy(phase, 2).start()
            self.copy(phase, 1).wait_recv()
            self.copy(phase, 3).start()
        else:
            self.copy(phase, 2).wait_recv()
            self.copy(phase, 3).wait_recv()

    def drain(self):
        for phase in range(3):
            for which in range(4 if phase else 3):
                self.copy(phase, which).wait_send()


class Scatter:
    def __init__(self, buf, kind, third, coords, landings, send, recv, out):
        self.buf, self.kind, self.third, self.coords = buf, kind, third, coords
        self.landings, self.send, self.recv, self.sid, self.out = landings, send, recv, kind * 3 + third, out

    def block(self, phase, by, half):
        order = ORDERS[self.third][::-1]
        axis = order[phase]
        value = lax.rem(self.coords[axis] + by, 4)
        return block_of(self.buf, self.coords, self.kind, self.third, order[phase + 1 :], axis, value, half)

    def landing(self, phase, which):
        if phase == 2:
            return self.landings[4].at[self.sid, which]
        return self.landings[2 * phase + which // 2].at[self.sid, which % 2]

    def copy(self, phase, which):
        axis = ORDERS[self.third][::-1][phase]
        if phase == 2:
            block, to = self.block(2, which + 1, None), which + 1
        else:
            block, to = self.block(phase, (2, 2, 1, 3)[which], (0, 1, None, None)[which]), (1, 3)[which % 2]
        return pltpu.make_async_remote_copy(
            src_ref=block,
            dst_ref=self.landing(phase, which),
            send_sem=self.send.at[self.sid, phase, which],
            recv_sem=self.recv.at[self.sid, phase, which],
            device_id=device_at(moved(self.coords, axis, to)),
            device_id_type=MESH,
        )

    def step(self, number):
        phase, stage = number // 3, number % 3
        if phase == 2:
            if stage == 0:
                for which in range(3):
                    self.copy(2, which).start()
            elif stage == 2:
                total = self.block(2, 0, None)[...].astype(f32)
                for which in range(3):
                    self.copy(2, which).wait_recv()
                    total = total + self.landing(2, which)[...].astype(f32)
                self.out[pl.ds(self.kind * 48 + self.third * 16, 16), :] = total
        elif stage == 0:
            self.copy(phase, 0).start()
            self.copy(phase, 1).start()
        elif stage == 1:
            for which, by in ((0, 1), (1, 3)):
                self.copy(phase, which).wait_recv()
                mine = self.block(phase, by, which)
                mine[...] = (mine[...].astype(f32) + self.landing(phase, which)[...].astype(f32)).astype(bf16)
                self.copy(phase, 2 + which).start()
        else:
            self.copy(phase, 2).wait_recv()
            self.copy(phase, 3).wait_recv()
            mine = self.block(phase, 0, None)
            total = (
                mine[...].astype(f32)
                + self.landing(phase, 2)[...].astype(f32)
                + self.landing(phase, 3)[...].astype(f32)
            )
            mine[...] = total.astype(bf16)

    def drain(self):
        for phase in range(3):
            for which in range(4 if phase < 2 else 3):
                self.copy(phase, which).wait_send()


class AllSum:
    def __init__(self, stages, landings, coords, send, recv):
        self.stages, self.landings, self.coords, self.send, self.recv = stages, landings, coords, send, recv

    def copy(self, phase, which):
        return pltpu.make_async_remote_copy(
            src_ref=self.stages.at[phase],
            dst_ref=self.landings.at[phase, which],
            send_sem=self.send.at[phase, which],
            recv_sem=self.recv.at[phase, which],
            device_id=device_at(moved(self.coords, "xyz"[phase], which + 1)),
            device_id_type=MESH,
        )

    def start(self, phase):
        for which in range(3):
            self.copy(phase, which).start()

    def finish(self, phase):
        for which in range(3):
            self.copy(phase, which).wait_recv()
        total = self.stages[phase].astype(f32)
        for which in range(3):
            total = total + self.landings[phase, which].astype(f32)
        self.stages[phase + 1] = total.astype(self.stages.dtype)

    def drain(self):
        for phase in range(3):
            for which in range(3):
                self.copy(phase, which).wait_send()


LANDINGS = [
    pltpu.VMEM((9, 2, 2, 4, 16, 768), bf16),
    pltpu.VMEM((9, 2, 4, 4, 16, 768), bf16),
    pltpu.VMEM((9, 2, 2, 16, 768), bf16),
    pltpu.VMEM((9, 2, 4, 16, 768), bf16),
    pltpu.VMEM((9, 3, 16, 768), bf16),
]


SEQ, IMG, ROWS = 197, 208, 416
CHUNK = 32
UNROLL = 13
EPS = 1e-6


def nn(a, b):
    return jnp.dot(a, b, preferred_element_type=f32)


def nt(a, b):
    return lax.dot_general(a, b, (((1,), (1,)), ((), ())), preferred_element_type=f32)


def tn(a, b):
    return lax.dot_general(a, b, (((0,), (0,)), ((), ())), preferred_element_type=f32)


def normed(v):
    center = v - jnp.mean(v, -1, keepdims=True)
    inv = lax.rsqrt(jnp.mean(center * center, -1, keepdims=True) + EPS)
    return center * inv, inv


def norm_back(dn, xhat, inv, gain):
    scaled = dn * gain
    return inv * (scaled - jnp.mean(scaled, -1, keepdims=True)
                  - xhat * jnp.mean(scaled * xhat, -1, keepdims=True))


def fold(v):
    return jnp.sum(v.reshape(v.shape[0] // 8, 8, v.shape[1]), axis=0)


def row_loop(body, init=None):
    def step(i, carry):
        return body(pl.ds(pl.multiple_of(i * CHUNK, CHUNK), CHUNK), carry)
    return lax.fori_loop(0, ROWS // CHUNK, step, init, unroll=UNROLL)


def square(ref, kind, j, lo=0, hi=768):
    return ref[kind, j, :, :, :, lo:hi].reshape(768, hi - lo)


def forward_attention(r, hook=None):
    vec = r.vec

    def first_norm(rows, _):
        xhat, _inv = normed(r.x[rows, :].astype(f32))
        r.n1[rows, :] = (xhat * vec[8:9, :] + vec[9:10, :]).astype(bf16)
    row_loop(first_norm)

    low = lax.broadcasted_iota(jnp.int32, (IMG, 128), 1) < 64
    keyed = lax.broadcasted_iota(jnp.int32, (IMG, IMG), 0) < SEQ
    zero = jnp.zeros((IMG, 128), bf16)

    def head_group(t, _):
        r.q[t] = (nn(r.n1[...], square(r.w, 0, t, 0, 640)) + vec[pl.ds(10 + t, 1), 0:640]).astype(bf16)

        def image(i):
            rows = slice(i * IMG, (i + 1) * IMG)
            tq, tk, tv, t3, t4 = (r.q[t, rows, k * 128:(k + 1) * 128] for k in range(5))

            def probs(h, qs, ks):
                s = jnp.where(keyed, nt(ks, qs) * 0.125, -1e30)
                e = jnp.exp(s - jnp.max(s, 0, keepdims=True))
                p = (e * (1.0 / jnp.sum(e, 0, keepdims=True))).astype(bf16)
                r.p[(t * 2 + i) * 3 + h] = p
                return p
            p0 = probs(0, jnp.where(low, tq, zero), tk)
            p1 = probs(1, jnp.where(low, zero, tq), tk)
            p2 = probs(2, jnp.where(low, t3, zero), t4)
            tvt = tv.T
            o01 = jnp.concatenate([nn(tvt[0:64], p0), nn(tvt[64:128], p1)], 0).astype(bf16)
            o2 = jnp.concatenate([jnp.zeros((64, IMG), bf16), nn(t3.T[64:128], p2).astype(bf16)], 0)
            r.mx[t, rows, 0:128] = o2.T
            r.mx[t, rows, 128:256] = o01.T
        image(0)
        image(1)
        part = nt(r.mx[t], square(r.w, 0, t, 512, 768))

        @pl.when(t == 0)
        def _():
            r.acc[...] = part

        @pl.when(t > 0)
        def _():
            r.acc[...] += part
        if hook is not None:
            hook(t)
        return 0
    lax.fori_loop(0, 4, head_group, 0)


def forward_up(r):
    vec = r.vec

    def second_norm(rows, _):
        h1 = r.x[rows, :].astype(f32) + r.acc[rows, :] + vec[1:2, :]
        r.h1[rows, :] = h1
        xhat, _inv = normed(h1)
        r.n2[rows, :] = (xhat * vec[0:1, :] + vec[2:3, :]).astype(bf16)
        r.acc[rows, :] = h1 + vec[3:4, :]
    row_loop(second_norm)

    def hidden(j, _):
        up = square(r.w, 1, j)
        for c in range(3):
            cols = slice(c * 256, (c + 1) * 256)
            u = nt(r.n2[...], up[cols]) + vec[pl.ds(4 + j, 1), cols]
            cdf = 0.5 * (1.0 + lax.erf(u * 0.7071067811865476))
            r.act[j, :, cols] = (u * cdf).astype(bf16)
            r.gp[j, :, cols] = (cdf + u * (jnp.exp(-0.5 * u * u) * 0.3989422804014327)).astype(bf16)
        return 0
    lax.fori_loop(0, 4, hidden, 0)


def forward_down(r):
    def hidden(j, _):
        r.acc[...] += nn(r.act[j], square(r.w, 2, j))
        return 0
    lax.fori_loop(0, 4, hidden, 0)


def backward_ffn(r, hook=None):
    vec = r.vec
    dvec = r.dvec

    def hidden(j, _):
        down = square(r.w, 2, j)
        for c in range(3):
            cols = slice(c * 256, (c + 1) * 256)
            du = (nt(r.gy[...], down[cols]) * r.gp[j, :, cols].astype(f32)).astype(bf16)
            r.gp[j, :, cols] = du
            dvec[pl.ds(4 + j, 1), cols] = jnp.sum(du.astype(f32), 0, keepdims=True)
        part = nn(r.gp[j], square(r.w, 1, j))

        @pl.when(j == 0)
        def _():
            r.acc[...] = part

        @pl.when(j > 0)
        def _():
            r.acc[...] += part
        if hook is not None:
            hook(j)
        return 0
    lax.fori_loop(0, 4, hidden, 0)

    def norm_two(rows, sums):
        dn = r.acc[rows, :]
        gy = r.gy[rows, :].astype(f32)
        xhat, inv = normed(r.h1[rows, :])
        dh = gy + norm_back(dn, xhat, inv, vec[0:1, :])
        r.h1[rows, :] = dh
        gh = dh.astype(bf16)
        r.gh[rows, :] = gh
        return (sums[0] + fold(dn * xhat), sums[1] + fold(dn), sums[2] + fold(gh.astype(f32)), sums[3] + fold(gy))
    zero = jnp.zeros((8, 768), f32)
    sums = row_loop(norm_two, (zero,) * 4)
    for row, total in zip((0, 2, 1, 3), sums):
        dvec[row:row + 1, :] = jnp.sum(total, 0, keepdims=True)


def grads_down(r):
    def hidden(j, _):
        r.g[2, j] = tn(r.act[j], r.gy[...]).astype(bf16).reshape(4, 4, 48, 768)
        return 0
    lax.fori_loop(0, 4, hidden, 0)


def grads_up(r):
    def hidden(j, _):
        r.g[1, j] = tn(r.gp[j], r.n2[...]).astype(bf16).reshape(4, 4, 48, 768)
        return 0
    lax.fori_loop(0, 4, hidden, 0)


def backward_attention(r, hook=None):
    dvec = r.dvec
    low = lax.broadcasted_iota(jnp.int32, (IMG, 128), 1) < 64
    zero = jnp.zeros((IMG, 128), bf16)

    def head_group(t, _):
        r.dm[...] = nn(r.gh[...], square(r.w, 0, t, 512, 768)).astype(bf16)

        def image(i):
            rows = slice(i * IMG, (i + 1) * IMG)
            tq, tk, tv, t3, t4 = (r.q[t, rows, k * 128:(k + 1) * 128] for k in range(5))
            d4 = r.dm[rows, 0:128]
            d5 = r.dm[rows, 128:256]

            def head(h, d_full, d_masked, v, q, kt):
                p = r.p[(t * 2 + i) * 3 + h]
                pf = p.astype(f32)
                dv = nn(p, d_full)
                dp = nt(v, d_masked)
                ds = (pf * (dp - jnp.sum(dp * pf, 0, keepdims=True))).astype(bf16)
                return nn(kt, ds), nn(ds, q) * 0.125, dv
            tkt = tk.T
            dq0, dk0, dv0 = head(0, d5, jnp.where(low, d5, zero), tv, tq, tkt[0:64])
            dq1, dk1, dv1 = head(1, d5, jnp.where(low, zero, d5), tv, tq, tkt[64:128])
            dq2, dk2, dv2 = head(2, d4, jnp.where(low, zero, d4), t3, t3, t4.T[0:64])
            r.q[t, rows, 0:128] = (jnp.concatenate([dq0, dq1], 0) * 0.125).astype(bf16).T
            r.q[t, rows, 128:256] = jnp.where(low, dk0, dk1).astype(bf16)
            r.q[t, rows, 256:384] = jnp.where(low, dv0, dv1).astype(bf16)
            dq2 = jnp.concatenate([(dq2 * 0.125).astype(bf16), jnp.zeros((64, IMG), bf16)], 0).T
            r.q[t, rows, 384:512] = jnp.where(low, dq2, dv2.astype(bf16))
            r.q[t, rows, 512:640] = jnp.where(low, dk2, 0.0).astype(bf16)
        image(0)
        image(1)
        dvec[pl.ds(10 + t, 1), 0:640] = jnp.sum(r.q[t].astype(f32), 0, keepdims=True)
        part = nt(r.q[t], square(r.w, 0, t, 0, 640))

        @pl.when(t == 0)
        def _():
            r.acc[...] = part

        @pl.when(t > 0)
        def _():
            r.acc[...] += part
        if hook is not None:
            hook(t)
        return 0
    lax.fori_loop(0, 4, head_group, 0)


def grads_attention(r):
    def head_group(t, _):
        ga = tn(r.n1[...], r.q[t])
        go = tn(r.gh[...], r.mx[t])
        r.g[0, t, :, :, :, 0:512] = ga[:, 0:512].astype(bf16).reshape(4, 4, 48, 512)
        r.g[0, t, :, :, :, 512:640] = (ga[:, 512:640] + go[:, 0:128]).astype(bf16).reshape(4, 4, 48, 128)
        r.g[0, t, :, :, :, 640:768] = go[:, 128:256].astype(bf16).reshape(4, 4, 48, 128)
        return 0
    lax.fori_loop(0, 4, head_group, 0)


def backward_end(r):
    vec = r.vec
    dvec = r.dvec

    def norm_one(rows, sums):
        dn = r.acc[rows, :]
        xhat, inv = normed(r.x[rows, :].astype(f32))
        dx = r.h1[rows, :] + norm_back(dn, xhat, inv, vec[8:9, :])
        r.dx[rows, :] = dx.astype(bf16)
        return (sums[0] + fold(dn * xhat), sums[1] + fold(dn))
    zero = jnp.zeros((8, 768), f32)
    sums = row_loop(norm_one, (zero,) * 2)
    for row, total in zip((8, 9), sums):
        dvec[row:row + 1, :] = jnp.sum(total, 0, keepdims=True)


SLOTS = (3, 4, 4, 4, 48, 768)
BODY_SCRATCH = dict(
    x=pltpu.VMEM((ROWS, 768), bf16), n1=pltpu.VMEM((ROWS, 768), bf16), q=pltpu.VMEM((4, ROWS, 640), bf16),
    p=pltpu.VMEM((24, IMG, IMG), bf16), mx=pltpu.VMEM((4, ROWS, 256), bf16), acc=pltpu.VMEM((ROWS, 768), f32),
    h1=pltpu.VMEM((ROWS, 768), f32), n2=pltpu.VMEM((ROWS, 768), bf16), act=pltpu.VMEM((4, ROWS, 768), bf16),
    gp=pltpu.VMEM((4, ROWS, 768), bf16), gy=pltpu.VMEM((ROWS, 768), bf16), gh=pltpu.VMEM((ROWS, 768), bf16),
    dm=pltpu.VMEM((ROWS, 256), bf16), dx=pltpu.VMEM((ROWS, 768), bf16),
    vec=pltpu.VMEM((16, 768), f32), dvec=pltpu.VMEM((16, 768), f32),
    w=pltpu.VMEM(SLOTS, bf16), g=pltpu.VMEM(SLOTS, bf16),
)


NAMES = list(BODY_SCRATCH)


def layer_kernel(w_hbm, rows_hbm, vec_hbm, end_hbm, grad_hbm, dvec_hbm, *scratch):
    r = types.SimpleNamespace(**dict(zip(NAMES, scratch)))
    rest = scratch[len(NAMES) :]
    landings, out = rest[:5], r.h1
    stages, sum_landings = rest[5:8], rest[8:11]
    ag_send, ag_recv, rs_send, rs_recv, sum_send, sum_recv, link, local, ready = rest[11:]
    coords = place()
    first = lax.axis_index("pipe") == 0
    second = lax.axis_index("pipe") == 1
    enter(coords)

    own = [
        pltpu.make_async_copy(
            w_hbm.at[kind], r.w.at[(kind, *(coords[name] for name in LAYOUT[kind]))], local.at[kind]
        )
        for kind in range(3)
    ]
    for copy in own:
        copy.start()
    vec_in = pltpu.make_async_copy(vec_hbm, stages[0].at[0], local.at[3])
    vec_in.start()

    @pl.when(first)
    def _():
        copy = pltpu.make_async_copy(rows_hbm, r.x, local.at[4])
        copy.start()
        copy.wait()

    @pl.when(second)
    def _():
        copy = pltpu.make_async_copy(rows_hbm, r.gy, local.at[4])
        copy.start()
        copy.wait()

    for copy in own:
        copy.wait()
    vec_in.wait()

    gathers = [Gather(r.w, kind, third, coords, ag_send, ag_recv) for kind in range(3) for third in range(3)]
    sums = [AllSum(stages[k], sum_landings[k], coords, sum_send.at[k], sum_recv.at[k]) for k in range(3)]

    def each(movers, *numbers):
        for number in numbers:
            for mover in movers:
                mover.step(number)

    early, late = gathers[:3], gathers[3:]
    sums[0].start(0)
    each(early, 0)
    each(late, 0)
    sums[0].finish(0)
    sums[0].start(1)
    each(early, 1)
    each(late, 1)
    each(early, 2, 3)
    sums[0].finish(1)
    sums[0].start(2)
    each(late, 2, 3)
    each(early, 4)
    sums[0].finish(2)
    each(late, 4)
    each(early, 5)

    @pl.when(second)
    def _():
        each(late, 5)
        pl.semaphore_wait(ready, 1)

    each(early, 6)

    @pl.when(first)
    def _():
        each(late, 5)

    each(late, 6)
    each(early, 7, 8)

    @pl.when(first)
    def _():
        pl.semaphore_signal(ready, inc=1, device_id=sibling(), device_id_type=MESH)
        each(late, 7)

    r.vec[...] = stages[0][3].astype(f32)
    r.dvec[...] = jnp.zeros_like(r.dvec)

    up = pltpu.make_async_remote_copy(
        src_ref=r.dx, dst_ref=r.x, send_sem=link.at[0], recv_sem=link.at[1], device_id=sibling(), device_id_type=MESH
    )
    down = pltpu.make_async_remote_copy(
        src_ref=r.dx, dst_ref=r.gy, send_sem=link.at[2], recv_sem=link.at[3], device_id=sibling(), device_id_type=MESH
    )
    end = pltpu.make_async_copy(r.dx, end_hbm, local.at[5])

    @pl.when(second)
    def _():
        each(late, 7)
        up.wait_recv()

    forward_attention(r)
    each(gathers[3:6], 8)
    forward_up(r)
    each(gathers[6:], 8)
    forward_down(r)
    r.dx[...] = r.acc[...].astype(bf16)

    @pl.when(first)
    def _():
        up.start()

    @pl.when(second)
    def _():
        end.start()

    for gather in gathers:
        gather.drain()
    sums[0].drain()

    @pl.when(first)
    def _():
        up.wait_send()
        down.wait_recv()

    scatters = [
        Scatter(r.g, kind, third, coords, landings, rs_send, rs_recv, out) for kind in range(3) for third in range(3)
    ]
    sa, su, sd = scatters[:3], scatters[3:6], scatters[6:]
    grads_down(r)
    each(sd, 0)

    def during_ffn(j):
        @pl.when(j == 2)
        def _():
            each(sd, 1)

    backward_ffn(r, during_ffn)
    stages[1][0] = r.dvec[0:8, :]
    sums[1].start(0)
    grads_up(r)
    each(su, 0)

    def during_attention(t):
        @pl.when(t == 3)
        def _():
            sums[1].finish(0)
            sums[1].start(1)
            each(sd, 2, 3)
            each(su, 1)

    backward_attention(r, during_attention)

    @pl.when(second)
    def _():
        end.wait()

    backward_end(r)

    @pl.when(first)
    def _():
        end.start()

    @pl.when(second)
    def _():
        down.start()

    stages[2][0] = r.dvec[8:16, :]
    sums[2].start(0)
    grads_attention(r)
    sums[2].finish(0)
    sums[2].start(1)
    each(sa, 0)
    sums[1].finish(1)
    sums[1].start(2)
    each(sd, 4)
    each(su, 2, 3)
    sums[2].finish(1)
    sums[2].start(2)
    each(sa, 1)
    each(sd, 5, 6)
    each(su, 4)
    sums[1].finish(2)
    each(sa, 2, 3)
    each(sd, 7)
    each(su, 5, 6)
    sums[2].finish(2)
    each(sa, 4)
    each(sd, 8)
    each(su, 7)
    each(sa, 5, 6)
    each(su, 8)
    each(sa, 7, 8)
    copies = [
        pltpu.make_async_copy(out.at[pl.ds(0, 144)], grad_hbm, local.at[0]),
        pltpu.make_async_copy(stages[1].at[3], dvec_hbm.at[pl.ds(0, 8)], local.at[1]),
        pltpu.make_async_copy(stages[2].at[3], dvec_hbm.at[pl.ds(8, 8)], local.at[2]),
    ]
    for copy in copies:
        copy.start()
    for scatter in scatters:
        scatter.drain()
    for some in sums[1:]:
        some.drain()

    @pl.when(first)
    def _():
        end.wait()

    @pl.when(second)
    def _():
        down.wait_send()

    for copy in copies:
        copy.wait()


def units(q, k, v, o):
    order = ((q, 0), (q, 1), (k, 0), (k, 1), (v, 0), (v, 1), (q, 2), (v, 2), (k, 2), (o, 2), (o, 0), (o, 1))
    return jnp.concatenate([a[..., h, :] for a, h in order], -1)


def split_units(joined):
    part = [joined[..., 64 * n : 64 * n + 64] for n in range(joined.shape[-1] // 64)]
    pick = lambda *numbers: jnp.stack([part[n] for n in numbers], -2)
    return pick(0, 1, 6), pick(2, 3, 8), pick(4, 5, 7), (pick(10, 11, 9) if len(part) > 10 else None)


def on_device(
    boundary, loads, norm_gains, row_biases, w_qkv, qv_bias, w_out, w_up, up_bias, w_down
):
    first = lax.axis_index("pipe") == 0
    fsdp, tp = lax.axis_index("fsdp"), lax.axis_index("tp")
    chip = fsdp * 4 + tp
    live = (tp < loads[:, 0])[:, None, None]
    rows = jnp.where(first | live, boundary[0], 0)
    rows = jnp.pad(rows, ((0, 0), (0, IMG - SEQ), (0, 0))).reshape(ROWS, 768)

    wq = w_qkv[0]
    wo = w_out[0].transpose(2, 0, 1)
    weights = jnp.stack([units(wq[:, 0], wq[:, 1], wq[:, 2], wo), w_up[0].T, w_down[0]], 0)

    lanes = jnp.arange(768, dtype=jnp.int32)
    gains, biases = norm_gains[0], row_biases[0]
    small = jnp.concatenate([gains[1:], biases[1:], gains[:1], biases[:1]], 0)
    small = jnp.where(lanes // 12 == chip, jnp.tile(small, (1, 64)), 0)
    hidden = jnp.arange(3072, dtype=jnp.int32)
    hidden = jnp.where(hidden // 48 == chip, jnp.tile(up_bias[0], 64), 0).reshape(4, 768)
    heads = jnp.where(
        jnp.arange(64, dtype=jnp.int32) // 4 == fsdp, jnp.tile(qv_bias[0], (1, 1, 16)), 0
    )
    none = jnp.zeros_like(heads[0])
    heads = units(heads[0], none, heads[1], none)
    heads = jnp.where(jnp.arange(4, dtype=jnp.int32)[:, None] == tp, heads[None], 0)
    vec = jnp.concatenate([small[:4], hidden, small[4:], heads, jnp.zeros((2, 768), bf16)], 0)

    anywhere = pl.BlockSpec(memory_space=pl.ANY)
    dma = pltpu.SemaphoreType.DMA
    end, grads, dvec = pl.pallas_call(
        layer_kernel,
        out_shape=(
            jax.ShapeDtypeStruct((ROWS, 768), bf16),
            jax.ShapeDtypeStruct((144, 768), f32),
            jax.ShapeDtypeStruct((16, 768), f32),
        ),
        in_specs=[anywhere] * 3,
        out_specs=(anywhere,) * 3,
        scratch_shapes=[
            *BODY_SCRATCH.values(),
            *LANDINGS,
            pltpu.VMEM((4, 16, 768), bf16),
            pltpu.VMEM((4, 8, 768), f32),
            pltpu.VMEM((4, 8, 768), f32),
            pltpu.VMEM((3, 3, 16, 768), bf16),
            pltpu.VMEM((3, 3, 8, 768), f32),
            pltpu.VMEM((3, 3, 8, 768), f32),
            dma((9, 3, 4)),
            dma((9, 3, 4)),
            dma((9, 3, 4)),
            dma((9, 3, 4)),
            dma((3, 3, 3)),
            dma((3, 3, 3)),
            dma((4,)),
            dma((6,)),
            pltpu.SemaphoreType.REGULAR,
        ],
        compiler_params=pltpu.CompilerParams(
            collective_id=0, has_side_effects=True, vmem_limit_bytes=63 * 2**20
        ),
    )(weights, rows, vec)

    end = end.reshape(2, IMG, 768)[:, :SEQ]
    ends = jnp.where(first | live, end, 0)[None]
    gq, gk, gv, go = split_units(grads[:48])
    mine = lax.dynamic_slice(dvec, (0, chip * 12), (10, 12))
    up_row = lax.dynamic_slice(dvec[4:8].reshape(3072), (chip * 48,), (48,))
    head_row = lax.dynamic_slice(dvec, (10 + tp, 0), (1, 640))[0]
    hq, _, hv, _ = split_units(head_row)
    head_grads = lax.dynamic_slice(jnp.stack([hq, hv], 0), (0, 0, fsdp * 4), (2, 3, 4))
    return (
        ends,
        jnp.stack([mine[8], mine[0]], 0)[None],
        jnp.stack([mine[9], mine[1], mine[2], mine[3]], 0)[None],
        jnp.stack([gq, gk, gv], 1)[None],
        head_grads[None],
        go.transpose(1, 2, 0)[None],
        grads[48:96].T[None],
        up_row[None],
        grads[96:][None],
    )


def solution(mesh):
    placed = (
        P("pipe", None, ("fsdp", "tp"), None),
        P(None, "fsdp"),
        P("pipe", None, ("fsdp", "tp")),
        P("pipe", None, ("fsdp", "tp")),
        P("pipe", "fsdp", None, "tp", None),
        P("pipe", None, "tp", "fsdp"),
        P("pipe", "tp", None, "fsdp"),
        P("pipe", None, ("fsdp", "tp")),
        P("pipe", ("fsdp", "tp")),
        P("pipe", ("fsdp", "tp"), None),
    )
    return jax.shard_map(
        on_device,
        mesh=mesh,
        in_specs=placed,
        out_specs=(placed[0], *placed[2:]),
        check_vma=False,
    )
```

```python
import types

import jax
import jax.numpy as jnp
from jax import lax
from jax.experimental import pallas as pl
from jax.experimental.pallas import tpu as pltpu
from jax.sharding import PartitionSpec as P

MESH = pl.DeviceIdType.MESH
bf16 = jnp.bfloat16
f32 = jnp.float32


ORDERS = (("x", "y", "z"), ("y", "z", "x"), ("z", "x", "y"))
LAYOUT = (("x", "z", "y"), ("z", "y", "x"), ("z", "y", "x"))


def place():
    f = lax.axis_index("fsdp")
    return {"z": f // 4, "y": lax.rem(f, 4), "x": lax.axis_index("tp")}


def device_at(coords):
    return {"fsdp": coords["z"] * 4 + coords["y"], "tp": coords["x"]}


def moved(coords, axis, by):
    out = dict(coords)
    out[axis] = lax.rem(coords[axis] + by, 4)
    return out


def sibling():
    return {"pipe": 1 - lax.axis_index("pipe")}


def enter(coords):
    barrier = pltpu.get_barrier_semaphore()
    for axis in ("x", "y", "z"):
        for by in (1, 2, 3):
            pl.semaphore_signal(barrier, inc=1, device_id=device_at(moved(coords, axis, by)), device_id_type=MESH)
    pl.semaphore_signal(barrier, inc=1, device_id=sibling(), device_id_type=MESH)
    pl.semaphore_wait(barrier, 10)


def block_of(buf, coords, kind, third, free, axis, value, half):
    index, cols = [], slice(None)
    uncut = half is not None
    for name in LAYOUT[kind]:
        if name in free:
            index.append(pl.ds(half * 2, 2) if uncut else slice(None))
            uncut = False
        else:
            index.append(value if name == axis else coords[name])
    if uncut:
        cols = pl.ds(half * 384, 384)
    return buf.at[(kind, *index, pl.ds(third * 16, 16), cols)]


class Gather:
    def __init__(self, buf, kind, third, coords, send, recv):
        self.buf, self.kind, self.third, self.coords = buf, kind, third, coords
        self.send, self.recv, self.sid = send, recv, kind * 3 + third

    def copy(self, phase, which):
        order = ORDERS[self.third]
        axis = order[phase]
        me = self.coords[axis]
        if phase == 0:
            value, half, by = me, None, which + 1
        else:
            value = (me, me, lax.rem(me + 3, 4), lax.rem(me + 1, 4))[which]
            half, by = (None, None, 0, 1)[which], (1, 3)[which % 2]
        ref = block_of(self.buf, self.coords, self.kind, self.third, order[:phase], axis, value, half)
        return pltpu.make_async_remote_copy(
            src_ref=ref,
            dst_ref=ref,
            send_sem=self.send.at[self.sid, phase, which],
            recv_sem=self.recv.at[self.sid, phase, which],
            device_id=device_at(moved(self.coords, axis, by)),
            device_id_type=MESH,
        )

    def step(self, number):
        phase, stage = number // 3, number % 3
        if phase == 0:
            for which in range(3):
                if stage == 0:
                    self.copy(0, which).start()
                elif stage == 2:
                    self.copy(0, which).wait_recv()
        elif stage == 0:
            self.copy(phase, 0).start()
            self.copy(phase, 1).start()
        elif stage == 1:
            self.copy(phase, 0).wait_recv()
            self.copy(phase, 2).start()
            self.copy(phase, 1).wait_recv()
            self.copy(phase, 3).start()
        else:
            self.copy(phase, 2).wait_recv()
            self.copy(phase, 3).wait_recv()

    def drain(self):
        for phase in range(3):
            for which in range(4 if phase else 3):
                self.copy(phase, which).wait_send()


class Scatter:
    def __init__(self, buf, kind, third, coords, landings, send, recv, out):
        self.buf, self.kind, self.third, self.coords = buf, kind, third, coords
        self.landings, self.send, self.recv, self.sid, self.out = landings, send, recv, kind * 3 + third, out

    def block(self, phase, by, half):
        order = ORDERS[self.third][::-1]
        axis = order[phase]
        value = lax.rem(self.coords[axis] + by, 4)
        return block_of(self.buf, self.coords, self.kind, self.third, order[phase + 1 :], axis, value, half)

    def landing(self, phase, which):
        if phase == 2:
            return self.landings[4].at[self.sid, which]
        return self.landings[2 * phase + which // 2].at[self.sid, which % 2]

    def copy(self, phase, which):
        axis = ORDERS[self.third][::-1][phase]
        if phase == 2:
            block, to = self.block(2, which + 1, None), which + 1
        else:
            block, to = self.block(phase, (2, 2, 1, 3)[which], (0, 1, None, None)[which]), (1, 3)[which % 2]
        return pltpu.make_async_remote_copy(
            src_ref=block,
            dst_ref=self.landing(phase, which),
            send_sem=self.send.at[self.sid, phase, which],
            recv_sem=self.recv.at[self.sid, phase, which],
            device_id=device_at(moved(self.coords, axis, to)),
            device_id_type=MESH,
        )

    def step(self, number):
        phase, stage = number // 3, number % 3
        if phase == 2:
            if stage == 0:
                for which in range(3):
                    self.copy(2, which).start()
            elif stage == 2:
                total = self.block(2, 0, None)[...].astype(f32)
                for which in range(3):
                    self.copy(2, which).wait_recv()
                    total = total + self.landing(2, which)[...].astype(f32)
                self.out[pl.ds(self.kind * 48 + self.third * 16, 16), :] = total
        elif stage == 0:
            self.copy(phase, 0).start()
            self.copy(phase, 1).start()
        elif stage == 1:
            for which, by in ((0, 1), (1, 3)):
                self.copy(phase, which).wait_recv()
                mine = self.block(phase, by, which)
                mine[...] = (mine[...].astype(f32) + self.landing(phase, which)[...].astype(f32)).astype(bf16)
                self.copy(phase, 2 + which).start()
        else:
            self.copy(phase, 2).wait_recv()
            self.copy(phase, 3).wait_recv()
            mine = self.block(phase, 0, None)
            total = (
                mine[...].astype(f32)
                + self.landing(phase, 2)[...].astype(f32)
                + self.landing(phase, 3)[...].astype(f32)
            )
            mine[...] = total.astype(bf16)

    def drain(self):
        for phase in range(3):
            for which in range(4 if phase < 2 else 3):
                self.copy(phase, which).wait_send()


class AllSum:
    def __init__(self, stages, landings, coords, send, recv):
        self.stages, self.landings, self.coords, self.send, self.recv = stages, landings, coords, send, recv

    def copy(self, phase, which):
        return pltpu.make_async_remote_copy(
            src_ref=self.stages.at[phase],
            dst_ref=self.landings.at[phase, which],
            send_sem=self.send.at[phase, which],
            recv_sem=self.recv.at[phase, which],
            device_id=device_at(moved(self.coords, "xyz"[phase], which + 1)),
            device_id_type=MESH,
        )

    def start(self, phase):
        for which in range(3):
            self.copy(phase, which).start()

    def finish(self, phase):
        for which in range(3):
            self.copy(phase, which).wait_recv()
        total = self.stages[phase].astype(f32)
        for which in range(3):
            total = total + self.landings[phase, which].astype(f32)
        self.stages[phase + 1] = total.astype(self.stages.dtype)

    def drain(self):
        for phase in range(3):
            for which in range(3):
                self.copy(phase, which).wait_send()


LANDINGS = [
    pltpu.VMEM((9, 2, 2, 4, 16, 768), bf16),
    pltpu.VMEM((9, 2, 4, 4, 16, 768), bf16),
    pltpu.VMEM((9, 2, 2, 16, 768), bf16),
    pltpu.VMEM((9, 2, 4, 16, 768), bf16),
    pltpu.VMEM((9, 3, 16, 768), bf16),
]


SEQ, IMG, ROWS = 197, 208, 416
CHUNK = 32
UNROLL = 13
EPS = 1e-6


def nn(a, b):
    return jnp.dot(a, b, preferred_element_type=f32)


def nt(a, b):
    return lax.dot_general(a, b, (((1,), (1,)), ((), ())), preferred_element_type=f32)


def tn(a, b):
    return lax.dot_general(a, b, (((0,), (0,)), ((), ())), preferred_element_type=f32)


def normed(v):
    center = v - jnp.mean(v, -1, keepdims=True)
    inv = lax.rsqrt(jnp.mean(center * center, -1, keepdims=True) + EPS)
    return center * inv, inv


def norm_back(dn, xhat, inv, gain):
    scaled = dn * gain
    return inv * (scaled - jnp.mean(scaled, -1, keepdims=True)
                  - xhat * jnp.mean(scaled * xhat, -1, keepdims=True))


def fold(v):
    return jnp.sum(v.reshape(v.shape[0] // 8, 8, v.shape[1]), axis=0)


def row_loop(body, init=None):
    def step(i, carry):
        return body(pl.ds(pl.multiple_of(i * CHUNK, CHUNK), CHUNK), carry)
    return lax.fori_loop(0, ROWS // CHUNK, step, init, unroll=UNROLL)


def square(ref, kind, j, lo=0, hi=768):
    return ref[kind, j, :, :, :, lo:hi].reshape(768, hi - lo)


def forward_attention(r, hook=None):
    vec = r.vec

    def first_norm(rows, _):
        xhat, _inv = normed(r.x[rows, :].astype(f32))
        r.n1[rows, :] = (xhat * vec[8:9, :] + vec[9:10, :]).astype(bf16)
    row_loop(first_norm)

    low = lax.broadcasted_iota(jnp.int32, (IMG, 128), 1) < 64
    keyed = lax.broadcasted_iota(jnp.int32, (IMG, IMG), 0) < SEQ
    zero = jnp.zeros((IMG, 128), bf16)

    def head_group(t, _):
        r.q[t] = (nn(r.n1[...], square(r.w, 0, t, 0, 640)) + vec[pl.ds(10 + t, 1), 0:640]).astype(bf16)

        def image(i):
            rows = slice(i * IMG, (i + 1) * IMG)
            tq, tk, tv, t3, t4 = (r.q[t, rows, k * 128:(k + 1) * 128] for k in range(5))

            def probs(h, qs, ks):
                s = jnp.where(keyed, nt(ks, qs) * 0.125, -1e30)
                e = jnp.exp(s - jnp.max(s, 0, keepdims=True))
                p = (e * (1.0 / jnp.sum(e, 0, keepdims=True))).astype(bf16)
                r.p[(t * 2 + i) * 3 + h] = p
                return p
            p0 = probs(0, jnp.where(low, tq, zero), tk)
            p1 = probs(1, jnp.where(low, zero, tq), tk)
            p2 = probs(2, jnp.where(low, t3, zero), t4)
            tvt = tv.T
            o01 = jnp.concatenate([nn(tvt[0:64], p0), nn(tvt[64:128], p1)], 0).astype(bf16)
            o2 = jnp.concatenate([jnp.zeros((64, IMG), bf16), nn(t3.T[64:128], p2).astype(bf16)], 0)
            r.mx[t, rows, 0:128] = o2.T
            r.mx[t, rows, 128:256] = o01.T
        image(0)
        image(1)
        part = nt(r.mx[t], square(r.w, 0, t, 512, 768))

        @pl.when(t == 0)
        def _():
            r.acc[...] = part

        @pl.when(t > 0)
        def _():
            r.acc[...] += part
        if hook is not None:
            hook(t)
        return 0
    lax.fori_loop(0, 4, head_group, 0)


def forward_up(r):
    vec = r.vec

    def second_norm(rows, _):
        h1 = r.x[rows, :].astype(f32) + r.acc[rows, :] + vec[1:2, :]
        r.h1[rows, :] = h1
        xhat, _inv = normed(h1)
        r.n2[rows, :] = (xhat * vec[0:1, :] + vec[2:3, :]).astype(bf16)
        r.acc[rows, :] = h1 + vec[3:4, :]
    row_loop(second_norm)

    def hidden(j, _):
        up = square(r.w, 1, j)
        for c in range(3):
            cols = slice(c * 256, (c + 1) * 256)
            u = nt(r.n2[...], up[cols]) + vec[pl.ds(4 + j, 1), cols]
            cdf = 0.5 * (1.0 + lax.erf(u * 0.7071067811865476))
            r.act[j, :, cols] = (u * cdf).astype(bf16)
            r.gp[j, :, cols] = (cdf + u * (jnp.exp(-0.5 * u * u) * 0.3989422804014327)).astype(bf16)
        return 0
    lax.fori_loop(0, 4, hidden, 0)


def forward_down(r):
    def hidden(j, _):
        r.acc[...] += nn(r.act[j], square(r.w, 2, j))
        return 0
    lax.fori_loop(0, 4, hidden, 0)


def backward_ffn(r, hook=None):
    vec = r.vec
    dvec = r.dvec

    def hidden(j, _):
        down = square(r.w, 2, j)
        for c in range(3):
            cols = slice(c * 256, (c + 1) * 256)
            du = (nt(r.gy[...], down[cols]) * r.gp[j, :, cols].astype(f32)).astype(bf16)
            r.gp[j, :, cols] = du
            dvec[pl.ds(4 + j, 1), cols] = jnp.sum(du.astype(f32), 0, keepdims=True)
        part = nn(r.gp[j], square(r.w, 1, j))

        @pl.when(j == 0)
        def _():
            r.acc[...] = part

        @pl.when(j > 0)
        def _():
            r.acc[...] += part
        if hook is not None:
            hook(j)
        return 0
    lax.fori_loop(0, 4, hidden, 0)

    def norm_two(rows, sums):
        dn = r.acc[rows, :]
        gy = r.gy[rows, :].astype(f32)
        xhat, inv = normed(r.h1[rows, :])
        dh = gy + norm_back(dn, xhat, inv, vec[0:1, :])
        r.h1[rows, :] = dh
        gh = dh.astype(bf16)
        r.gh[rows, :] = gh
        return (sums[0] + fold(dn * xhat), sums[1] + fold(dn), sums[2] + fold(gh.astype(f32)), sums[3] + fold(gy))
    zero = jnp.zeros((8, 768), f32)
    sums = row_loop(norm_two, (zero,) * 4)
    for row, total in zip((0, 2, 1, 3), sums):
        dvec[row:row + 1, :] = jnp.sum(total, 0, keepdims=True)


def grads_down(r):
    def hidden(j, _):
        r.g[2, j] = tn(r.act[j], r.gy[...]).astype(bf16).reshape(4, 4, 48, 768)
        return 0
    lax.fori_loop(0, 4, hidden, 0)


def grads_up(r):
    def hidden(j, _):
        r.g[1, j] = tn(r.gp[j], r.n2[...]).astype(bf16).reshape(4, 4, 48, 768)
        return 0
    lax.fori_loop(0, 4, hidden, 0)


def backward_attention(r, hook=None):
    dvec = r.dvec
    low = lax.broadcasted_iota(jnp.int32, (IMG, 128), 1) < 64
    zero = jnp.zeros((IMG, 128), bf16)

    def head_group(t, _):
        r.dm[...] = nn(r.gh[...], square(r.w, 0, t, 512, 768)).astype(bf16)

        def image(i):
            rows = slice(i * IMG, (i + 1) * IMG)
            tq, tk, tv, t3, t4 = (r.q[t, rows, k * 128:(k + 1) * 128] for k in range(5))
            d4 = r.dm[rows, 0:128]
            d5 = r.dm[rows, 128:256]

            def head(h, d_full, d_masked, v, q, kt):
                p = r.p[(t * 2 + i) * 3 + h]
                pf = p.astype(f32)
                dv = nn(p, d_full)
                dp = nt(v, d_masked)
                ds = (pf * (dp - jnp.sum(dp * pf, 0, keepdims=True))).astype(bf16)
                return nn(kt, ds), nn(ds, q) * 0.125, dv
            tkt = tk.T
            dq0, dk0, dv0 = head(0, d5, jnp.where(low, d5, zero), tv, tq, tkt[0:64])
            dq1, dk1, dv1 = head(1, d5, jnp.where(low, zero, d5), tv, tq, tkt[64:128])
            dq2, dk2, dv2 = head(2, d4, jnp.where(low, zero, d4), t3, t3, t4.T[0:64])
            r.q[t, rows, 0:128] = (jnp.concatenate([dq0, dq1], 0) * 0.125).astype(bf16).T
            r.q[t, rows, 128:256] = jnp.where(low, dk0, dk1).astype(bf16)
            r.q[t, rows, 256:384] = jnp.where(low, dv0, dv1).astype(bf16)
            dq2 = jnp.concatenate([(dq2 * 0.125).astype(bf16), jnp.zeros((64, IMG), bf16)], 0).T
            r.q[t, rows, 384:512] = jnp.where(low, dq2, dv2.astype(bf16))
            r.q[t, rows, 512:640] = jnp.where(low, dk2, 0.0).astype(bf16)
        image(0)
        image(1)
        dvec[pl.ds(10 + t, 1), 0:640] = jnp.sum(r.q[t].astype(f32), 0, keepdims=True)
        part = nt(r.q[t], square(r.w, 0, t, 0, 640))

        @pl.when(t == 0)
        def _():
            r.acc[...] = part

        @pl.when(t > 0)
        def _():
            r.acc[...] += part
        if hook is not None:
            hook(t)
        return 0
    lax.fori_loop(0, 4, head_group, 0)


def grads_attention(r):
    def head_group(t, _):
        ga = tn(r.n1[...], r.q[t])
        go = tn(r.gh[...], r.mx[t])
        r.g[0, t, :, :, :, 0:512] = ga[:, 0:512].astype(bf16).reshape(4, 4, 48, 512)
        r.g[0, t, :, :, :, 512:640] = (ga[:, 512:640] + go[:, 0:128]).astype(bf16).reshape(4, 4, 48, 128)
        r.g[0, t, :, :, :, 640:768] = go[:, 128:256].astype(bf16).reshape(4, 4, 48, 128)
        return 0
    lax.fori_loop(0, 4, head_group, 0)


def backward_end(r):
    vec = r.vec
    dvec = r.dvec

    def norm_one(rows, sums):
        dn = r.acc[rows, :]
        xhat, inv = normed(r.x[rows, :].astype(f32))
        dx = r.h1[rows, :] + norm_back(dn, xhat, inv, vec[8:9, :])
        r.dx[rows, :] = dx.astype(bf16)
        return (sums[0] + fold(dn * xhat), sums[1] + fold(dn))
    zero = jnp.zeros((8, 768), f32)
    sums = row_loop(norm_one, (zero,) * 2)
    for row, total in zip((8, 9), sums):
        dvec[row:row + 1, :] = jnp.sum(total, 0, keepdims=True)


SLOTS = (3, 4, 4, 4, 48, 768)
BODY_SCRATCH = dict(
    x=pltpu.VMEM((ROWS, 768), bf16), n1=pltpu.VMEM((ROWS, 768), bf16), q=pltpu.VMEM((4, ROWS, 640), bf16),
    p=pltpu.VMEM((24, IMG, IMG), bf16), mx=pltpu.VMEM((4, ROWS, 256), bf16), acc=pltpu.VMEM((ROWS, 768), f32),
    h1=pltpu.VMEM((ROWS, 768), f32), n2=pltpu.VMEM((ROWS, 768), bf16), act=pltpu.VMEM((4, ROWS, 768), bf16),
    gp=pltpu.VMEM((4, ROWS, 768), bf16), gy=pltpu.VMEM((ROWS, 768), bf16), gh=pltpu.VMEM((ROWS, 768), bf16),
    dm=pltpu.VMEM((ROWS, 256), bf16), dx=pltpu.VMEM((ROWS, 768), bf16),
    vec=pltpu.VMEM((16, 768), f32), dvec=pltpu.VMEM((16, 768), f32),
    w=pltpu.VMEM(SLOTS, bf16), g=pltpu.VMEM(SLOTS, bf16),
)


NAMES = list(BODY_SCRATCH)


def layer_kernel(w_hbm, rows_hbm, vec_hbm, end_hbm, grad_hbm, dvec_hbm, *scratch):
    r = types.SimpleNamespace(**dict(zip(NAMES, scratch)))
    rest = scratch[len(NAMES) :]
    landings, out = rest[:5], r.h1
    stages, sum_landings = rest[5:8], rest[8:11]
    ag_send, ag_recv, rs_send, rs_recv, sum_send, sum_recv, link, local, ready = rest[11:]
    coords = place()
    first = lax.axis_index("pipe") == 0
    second = lax.axis_index("pipe") == 1
    own = [
        pltpu.make_async_copy(
            w_hbm.at[kind], r.w.at[(kind, *(coords[name] for name in LAYOUT[kind]))], local.at[kind]
        )
        for kind in range(3)
    ]
    for copy in own:
        copy.start()
    vec_in = pltpu.make_async_copy(vec_hbm, stages[0].at[0], local.at[3])
    vec_in.start()

    to_x = pltpu.make_async_copy(rows_hbm, r.x, local.at[4])
    to_gy = pltpu.make_async_copy(rows_hbm, r.gy, local.at[4])

    @pl.when(first)
    def _():
        to_x.start()

    @pl.when(second)
    def _():
        to_gy.start()

    enter(coords)
    for copy in own:
        copy.wait()
    vec_in.wait()

    gathers = [Gather(r.w, kind, third, coords, ag_send, ag_recv) for kind in range(3) for third in range(3)]
    sums = [AllSum(stages[k], sum_landings[k], coords, sum_send.at[k], sum_recv.at[k]) for k in range(3)]

    def each(movers, *numbers):
        for number in numbers:
            for mover in movers:
                mover.step(number)

    early, late = gathers[:3], gathers[3:]
    sums[0].start(0)
    each(early, 0)
    each(late, 0)
    sums[0].finish(0)
    sums[0].start(1)
    each(early, 1)
    each(late, 1)
    each(early, 2, 3)
    sums[0].finish(1)
    sums[0].start(2)
    each(late, 2, 3)
    each(early, 4)
    sums[0].finish(2)
    each(late, 4)
    each(early, 5)

    @pl.when(second)
    def _():
        each(late, 5)
        pl.semaphore_wait(ready, 1)

    each(early, 6)

    @pl.when(first)
    def _():
        each(late, 5)

    each(late, 6)
    each(early, 7, 8)

    @pl.when(first)
    def _():
        pl.semaphore_signal(ready, inc=1, device_id=sibling(), device_id_type=MESH)
        each(late, 7)

    r.vec[...] = stages[0][3].astype(f32)
    r.dvec[...] = jnp.zeros_like(r.dvec)

    up = pltpu.make_async_remote_copy(
        src_ref=r.dx, dst_ref=r.x, send_sem=link.at[0], recv_sem=link.at[1], device_id=sibling(), device_id_type=MESH
    )
    down = pltpu.make_async_remote_copy(
        src_ref=r.dx, dst_ref=r.gy, send_sem=link.at[2], recv_sem=link.at[3], device_id=sibling(), device_id_type=MESH
    )
    end = pltpu.make_async_copy(r.dx, end_hbm, local.at[5])

    @pl.when(first)
    def _():
        to_x.wait()

    @pl.when(second)
    def _():
        to_gy.wait()
        each(late, 7)
        up.wait_recv()

    forward_attention(r)
    each(gathers[3:6], 8)
    forward_up(r)
    each(gathers[6:], 8)
    forward_down(r)
    r.dx[...] = r.acc[...].astype(bf16)

    @pl.when(first)
    def _():
        up.start()

    @pl.when(second)
    def _():
        end.start()

    for gather in gathers:
        gather.drain()
    sums[0].drain()

    @pl.when(first)
    def _():
        up.wait_send()
        down.wait_recv()

    scatters = [
        Scatter(r.g, kind, third, coords, landings, rs_send, rs_recv, out) for kind in range(3) for third in range(3)
    ]
    sa, su, sd = scatters[:3], scatters[3:6], scatters[6:]
    grads_down(r)
    each(sd, 0)

    def during_ffn(j):
        @pl.when(j == 2)
        def _():
            each(sd, 1)

    backward_ffn(r, during_ffn)
    stages[1][0] = r.dvec[0:8, :]
    sums[1].start(0)
    grads_up(r)
    each(su, 0)

    def during_attention(t):
        @pl.when(t == 3)
        def _():
            sums[1].finish(0)
            sums[1].start(1)
            each(sd, 2, 3)
            each(su, 1)

    backward_attention(r, during_attention)

    @pl.when(second)
    def _():
        end.wait()

    backward_end(r)

    @pl.when(first)
    def _():
        end.start()

    @pl.when(second)
    def _():
        down.start()

    stages[2][0] = r.dvec[8:16, :]
    sums[2].start(0)
    grads_attention(r)
    sums[2].finish(0)
    sums[2].start(1)
    each(sa, 0)
    sums[1].finish(1)
    sums[1].start(2)
    each(sd, 4)
    each(su, 2, 3)
    sums[2].finish(1)
    sums[2].start(2)
    each(sa, 1)
    each(sd, 5, 6)
    each(su, 4)
    sums[1].finish(2)
    each(sa, 2, 3)
    each(sd, 7)
    each(su, 5, 6)
    sums[2].finish(2)
    each(sa, 4)
    each(sd, 8)
    each(su, 7)
    each(sa, 5, 6)
    each(su, 8)
    each(sa, 7, 8)
    copies = [
        pltpu.make_async_copy(out.at[pl.ds(0, 144)], grad_hbm, local.at[0]),
        pltpu.make_async_copy(stages[1].at[3], dvec_hbm.at[pl.ds(0, 8)], local.at[1]),
        pltpu.make_async_copy(stages[2].at[3], dvec_hbm.at[pl.ds(8, 8)], local.at[2]),
    ]
    for copy in copies:
        copy.start()
    for scatter in scatters:
        scatter.drain()
    for some in sums[1:]:
        some.drain()

    @pl.when(first)
    def _():
        end.wait()

    @pl.when(second)
    def _():
        down.wait_send()

    for copy in copies:
        copy.wait()


def units(q, k, v, o):
    order = ((q, 0), (q, 1), (k, 0), (k, 1), (v, 0), (v, 1), (q, 2), (v, 2), (k, 2), (o, 2), (o, 0), (o, 1))
    return jnp.concatenate([a[..., h, :] for a, h in order], -1)


def split_units(joined):
    part = [joined[..., 64 * n : 64 * n + 64] for n in range(joined.shape[-1] // 64)]
    pick = lambda *numbers: jnp.stack([part[n] for n in numbers], -2)
    return pick(0, 1, 6), pick(2, 3, 8), pick(4, 5, 7), (pick(10, 11, 9) if len(part) > 10 else None)


def on_device(
    boundary, loads, norm_gains, row_biases, w_qkv, qv_bias, w_out, w_up, up_bias, w_down
):
    first = lax.axis_index("pipe") == 0
    fsdp, tp = lax.axis_index("fsdp"), lax.axis_index("tp")
    chip = fsdp * 4 + tp
    live = (tp < loads[:, 0])[:, None, None]
    rows = jnp.where(first | live, boundary[0], 0)
    rows = jnp.pad(rows, ((0, 0), (0, IMG - SEQ), (0, 0))).reshape(ROWS, 768)

    wq = w_qkv[0]
    wo = w_out[0].transpose(2, 0, 1)
    weights = jnp.stack([units(wq[:, 0], wq[:, 1], wq[:, 2], wo), w_up[0].T, w_down[0]], 0)

    lanes = jnp.arange(768, dtype=jnp.int32)
    gains, biases = norm_gains[0], row_biases[0]
    small = jnp.concatenate([gains[1:], biases[1:], gains[:1], biases[:1]], 0)
    small = jnp.where(lanes // 12 == chip, jnp.tile(small, (1, 64)), 0)
    hidden = jnp.arange(3072, dtype=jnp.int32)
    hidden = jnp.where(hidden // 48 == chip, jnp.tile(up_bias[0], 64), 0).reshape(4, 768)
    heads = jnp.where(
        jnp.arange(64, dtype=jnp.int32) // 4 == fsdp, jnp.tile(qv_bias[0], (1, 1, 16)), 0
    )
    none = jnp.zeros_like(heads[0])
    heads = units(heads[0], none, heads[1], none)
    heads = jnp.where(jnp.arange(4, dtype=jnp.int32)[:, None] == tp, heads[None], 0)
    vec = jnp.concatenate([small[:4], hidden, small[4:], heads, jnp.zeros((2, 768), bf16)], 0)

    anywhere = pl.BlockSpec(memory_space=pl.ANY)
    dma = pltpu.SemaphoreType.DMA
    end, grads, dvec = pl.pallas_call(
        layer_kernel,
        out_shape=(
            jax.ShapeDtypeStruct((ROWS, 768), bf16),
            jax.ShapeDtypeStruct((144, 768), f32),
            jax.ShapeDtypeStruct((16, 768), f32),
        ),
        in_specs=[anywhere] * 3,
        out_specs=(anywhere,) * 3,
        scratch_shapes=[
            *BODY_SCRATCH.values(),
            *LANDINGS,
            pltpu.VMEM((4, 16, 768), bf16),
            pltpu.VMEM((4, 8, 768), f32),
            pltpu.VMEM((4, 8, 768), f32),
            pltpu.VMEM((3, 3, 16, 768), bf16),
            pltpu.VMEM((3, 3, 8, 768), f32),
            pltpu.VMEM((3, 3, 8, 768), f32),
            dma((9, 3, 4)),
            dma((9, 3, 4)),
            dma((9, 3, 4)),
            dma((9, 3, 4)),
            dma((3, 3, 3)),
            dma((3, 3, 3)),
            dma((4,)),
            dma((6,)),
            pltpu.SemaphoreType.REGULAR,
        ],
        compiler_params=pltpu.CompilerParams(
            collective_id=0, has_side_effects=True, vmem_limit_bytes=63 * 2**20
        ),
    )(weights, rows, vec)

    end = end.reshape(2, IMG, 768)[:, :SEQ]
    ends = jnp.where(first | live, end, 0)[None]
    gq, gk, gv, go = split_units(grads[:48])
    mine = lax.dynamic_slice(dvec, (0, chip * 12), (10, 12))
    up_row = lax.dynamic_slice(dvec[4:8].reshape(3072), (chip * 48,), (48,))
    head_row = lax.dynamic_slice(dvec, (10 + tp, 0), (1, 640))[0]
    hq, _, hv, _ = split_units(head_row)
    head_grads = lax.dynamic_slice(jnp.stack([hq, hv], 0), (0, 0, fsdp * 4), (2, 3, 4))
    return (
        ends,
        jnp.stack([mine[8], mine[0]], 0)[None],
        jnp.stack([mine[9], mine[1], mine[2], mine[3]], 0)[None],
        jnp.stack([gq, gk, gv], 1)[None],
        head_grads[None],
        go.transpose(1, 2, 0)[None],
        grads[48:96].T[None],
        up_row[None],
        grads[96:][None],
    )


def solution(mesh):
    placed = (
        P("pipe", None, ("fsdp", "tp"), None),
        P(None, "fsdp"),
        P("pipe", None, ("fsdp", "tp")),
        P("pipe", None, ("fsdp", "tp")),
        P("pipe", "fsdp", None, "tp", None),
        P("pipe", None, "tp", "fsdp"),
        P("pipe", "tp", None, "fsdp"),
        P("pipe", None, ("fsdp", "tp")),
        P("pipe", ("fsdp", "tp")),
        P("pipe", ("fsdp", "tp"), None),
    )
    return jax.shard_map(
        on_device,
        mesh=mesh,
        in_specs=placed,
        out_specs=(placed[0], *placed[2:]),
        check_vma=False,
    )
```

```python
import types

import jax
import jax.numpy as jnp
from jax import lax
from jax.experimental import pallas as pl
from jax.experimental.pallas import tpu as pltpu
from jax.sharding import PartitionSpec as P

MESH = pl.DeviceIdType.MESH
bf16 = jnp.bfloat16
f32 = jnp.float32


ORDERS = (("x", "y", "z"), ("y", "z", "x"), ("z", "x", "y"))
LAYOUT = (("x", "z", "y"), ("z", "y", "x"), ("z", "y", "x"))


def place():
    f = lax.axis_index("fsdp")
    return {"z": f // 4, "y": lax.rem(f, 4), "x": lax.axis_index("tp")}


def device_at(coords):
    return {"fsdp": coords["z"] * 4 + coords["y"], "tp": coords["x"]}


def moved(coords, axis, by):
    out = dict(coords)
    out[axis] = lax.rem(coords[axis] + by, 4)
    return out


def sibling():
    return {"pipe": 1 - lax.axis_index("pipe")}


def enter(coords):
    barrier = pltpu.get_barrier_semaphore()
    for axis in ("x", "y", "z"):
        for by in (1, 2, 3):
            pl.semaphore_signal(barrier, inc=1, device_id=device_at(moved(coords, axis, by)), device_id_type=MESH)
    pl.semaphore_signal(barrier, inc=1, device_id=sibling(), device_id_type=MESH)
    pl.semaphore_wait(barrier, 10)


def block_of(buf, coords, kind, third, free, axis, value, half):
    index, cols = [], slice(None)
    uncut = half is not None
    for name in LAYOUT[kind]:
        if name in free:
            index.append(pl.ds(half * 2, 2) if uncut else slice(None))
            uncut = False
        else:
            index.append(value if name == axis else coords[name])
    if uncut:
        cols = pl.ds(half * 384, 384)
    return buf.at[(kind, *index, pl.ds(third * 16, 16), cols)]


class Gather:
    def __init__(self, buf, kind, third, coords, send, recv):
        self.buf, self.kind, self.third, self.coords = buf, kind, third, coords
        self.send, self.recv, self.sid = send, recv, kind * 3 + third

    def copy(self, phase, which):
        order = ORDERS[self.third]
        axis = order[phase]
        me = self.coords[axis]
        if phase == 0:
            value, half, by = me, None, which + 1
        else:
            value = (me, me, lax.rem(me + 3, 4), lax.rem(me + 1, 4))[which]
            half, by = (None, None, 0, 1)[which], (1, 3)[which % 2]
        ref = block_of(self.buf, self.coords, self.kind, self.third, order[:phase], axis, value, half)
        return pltpu.make_async_remote_copy(
            src_ref=ref,
            dst_ref=ref,
            send_sem=self.send.at[self.sid, phase, which],
            recv_sem=self.recv.at[self.sid, phase, which],
            device_id=device_at(moved(self.coords, axis, by)),
            device_id_type=MESH,
        )

    def step(self, number):
        phase, stage = number // 3, number % 3
        if phase == 0:
            for which in range(3):
                if stage == 0:
                    self.copy(0, which).start()
                elif stage == 2:
                    self.copy(0, which).wait_recv()
        elif stage == 0:
            self.copy(phase, 0).start()
            self.copy(phase, 1).start()
        elif stage == 1:
            self.copy(phase, 0).wait_recv()
            self.copy(phase, 2).start()
            self.copy(phase, 1).wait_recv()
            self.copy(phase, 3).start()
        else:
            self.copy(phase, 2).wait_recv()
            self.copy(phase, 3).wait_recv()

    def drain(self):
        for phase in range(3):
            for which in range(4 if phase else 3):
                self.copy(phase, which).wait_send()


class Scatter:
    def __init__(self, buf, kind, third, coords, landings, send, recv, out):
        self.buf, self.kind, self.third, self.coords = buf, kind, third, coords
        self.landings, self.send, self.recv, self.sid, self.out = landings, send, recv, kind * 3 + third, out

    def block(self, phase, by, half):
        order = ORDERS[self.third][::-1]
        axis = order[phase]
        value = lax.rem(self.coords[axis] + by, 4)
        return block_of(self.buf, self.coords, self.kind, self.third, order[phase + 1 :], axis, value, half)

    def landing(self, phase, which):
        if phase == 2:
            return self.landings[4].at[self.sid, which]
        return self.landings[2 * phase + which // 2].at[self.sid, which % 2]

    def copy(self, phase, which):
        axis = ORDERS[self.third][::-1][phase]
        if phase == 2:
            block, to = self.block(2, which + 1, None), which + 1
        else:
            block, to = self.block(phase, (2, 2, 1, 3)[which], (0, 1, None, None)[which]), (1, 3)[which % 2]
        return pltpu.make_async_remote_copy(
            src_ref=block,
            dst_ref=self.landing(phase, which),
            send_sem=self.send.at[self.sid, phase, which],
            recv_sem=self.recv.at[self.sid, phase, which],
            device_id=device_at(moved(self.coords, axis, to)),
            device_id_type=MESH,
        )

    def step(self, number):
        phase, stage = number // 3, number % 3
        if phase == 2:
            if stage == 0:
                for which in range(3):
                    self.copy(2, which).start()
            elif stage == 2:
                total = self.block(2, 0, None)[...].astype(f32)
                for which in range(3):
                    self.copy(2, which).wait_recv()
                    total = total + self.landing(2, which)[...].astype(f32)
                self.out[pl.ds(self.kind * 48 + self.third * 16, 16), :] = total
        elif stage == 0:
            self.copy(phase, 0).start()
            self.copy(phase, 1).start()
        elif stage == 1:
            for which, by in ((0, 1), (1, 3)):
                self.copy(phase, which).wait_recv()
                mine = self.block(phase, by, which)
                mine[...] = (mine[...].astype(f32) + self.landing(phase, which)[...].astype(f32)).astype(bf16)
                self.copy(phase, 2 + which).start()
        else:
            self.copy(phase, 2).wait_recv()
            self.copy(phase, 3).wait_recv()
            mine = self.block(phase, 0, None)
            total = (
                mine[...].astype(f32)
                + self.landing(phase, 2)[...].astype(f32)
                + self.landing(phase, 3)[...].astype(f32)
            )
            mine[...] = total.astype(bf16)

    def drain(self):
        for phase in range(3):
            for which in range(4 if phase < 2 else 3):
                self.copy(phase, which).wait_send()


class AllSum:
    def __init__(self, stages, landings, coords, send, recv):
        self.stages, self.landings, self.coords, self.send, self.recv = stages, landings, coords, send, recv

    def copy(self, phase, which):
        return pltpu.make_async_remote_copy(
            src_ref=self.stages.at[phase],
            dst_ref=self.landings.at[phase, which],
            send_sem=self.send.at[phase, which],
            recv_sem=self.recv.at[phase, which],
            device_id=device_at(moved(self.coords, "xyz"[phase], which + 1)),
            device_id_type=MESH,
        )

    def start(self, phase):
        for which in range(3):
            self.copy(phase, which).start()

    def finish(self, phase):
        for which in range(3):
            self.copy(phase, which).wait_recv()
        total = self.stages[phase].astype(f32)
        for which in range(3):
            total = total + self.landings[phase, which].astype(f32)
        self.stages[phase + 1] = total.astype(self.stages.dtype)

    def drain(self):
        for phase in range(3):
            for which in range(3):
                self.copy(phase, which).wait_send()


LANDINGS = [
    pltpu.VMEM((9, 2, 2, 4, 16, 768), bf16),
    pltpu.VMEM((9, 2, 4, 4, 16, 768), bf16),
    pltpu.VMEM((9, 2, 2, 16, 768), bf16),
    pltpu.VMEM((9, 2, 4, 16, 768), bf16),
    pltpu.VMEM((9, 3, 16, 768), bf16),
]


SEQ, IMG, ROWS = 197, 208, 416
CHUNK = 32
UNROLL = 13
EPS = 1e-6


def nn(a, b):
    return jnp.dot(a, b, preferred_element_type=f32)


def nt(a, b):
    return lax.dot_general(a, b, (((1,), (1,)), ((), ())), preferred_element_type=f32)


def tn(a, b):
    return lax.dot_general(a, b, (((0,), (0,)), ((), ())), preferred_element_type=f32)


def normed(v):
    center = v - jnp.mean(v, -1, keepdims=True)
    inv = lax.rsqrt(jnp.mean(center * center, -1, keepdims=True) + EPS)
    return center * inv, inv


def norm_back(dn, xhat, inv, gain):
    scaled = dn * gain
    return inv * (scaled - jnp.mean(scaled, -1, keepdims=True)
                  - xhat * jnp.mean(scaled * xhat, -1, keepdims=True))


def fold(v):
    return jnp.sum(v.reshape(v.shape[0] // 8, 8, v.shape[1]), axis=0)


def row_loop(body, init=None):
    def step(i, carry):
        return body(pl.ds(pl.multiple_of(i * CHUNK, CHUNK), CHUNK), carry)
    return lax.fori_loop(0, ROWS // CHUNK, step, init, unroll=UNROLL)


def square(ref, kind, j, lo=0, hi=768):
    return ref[kind, j, :, :, :, lo:hi].reshape(768, hi - lo)


def forward_attention(r, hook=None):
    vec = r.vec

    def first_norm(rows, _):
        xhat, _inv = normed(r.x[rows, :].astype(f32))
        r.n1[rows, :] = (xhat * vec[8:9, :] + vec[9:10, :]).astype(bf16)
    row_loop(first_norm)

    low = lax.broadcasted_iota(jnp.int32, (IMG, 128), 1) < 64
    keyed = lax.broadcasted_iota(jnp.int32, (IMG, IMG), 0) < SEQ
    zero = jnp.zeros((IMG, 128), bf16)

    def head_group(t, _):
        r.q[t] = (nn(r.n1[...], square(r.w, 0, t, 0, 640)) + vec[pl.ds(10 + t, 1), 0:640]).astype(bf16)

        def image(i):
            rows = slice(i * IMG, (i + 1) * IMG)
            tq, tk, tv, t3, t4 = (r.q[t, rows, k * 128:(k + 1) * 128] for k in range(5))

            def probs(h, qs, ks):
                s = jnp.where(keyed, nt(ks, qs) * 0.125, -1e30)
                e = jnp.exp(s - jnp.max(s, 0, keepdims=True))
                p = (e * (1.0 / jnp.sum(e, 0, keepdims=True))).astype(bf16)
                r.p[(t * 2 + i) * 3 + h] = p
                return p
            p0 = probs(0, jnp.where(low, tq, zero), tk)
            p1 = probs(1, jnp.where(low, zero, tq), tk)
            p2 = probs(2, jnp.where(low, t3, zero), t4)
            tvt = tv.T
            o01 = jnp.concatenate([nn(tvt[0:64], p0), nn(tvt[64:128], p1)], 0).astype(bf16)
            o2 = jnp.concatenate([jnp.zeros((64, IMG), bf16), nn(t3.T[64:128], p2).astype(bf16)], 0)
            r.mx[t, rows, 0:128] = o2.T
            r.mx[t, rows, 128:256] = o01.T
        image(0)
        image(1)
        part = nt(r.mx[t], square(r.w, 0, t, 512, 768))

        @pl.when(t == 0)
        def _():
            r.acc[...] = part

        @pl.when(t > 0)
        def _():
            r.acc[...] += part
        if hook is not None:
            hook(t)
        return 0
    lax.fori_loop(0, 4, head_group, 0)


def forward_up(r):
    vec = r.vec

    def second_norm(rows, _):
        h1 = r.x[rows, :].astype(f32) + r.acc[rows, :] + vec[1:2, :]
        r.h1[rows, :] = h1
        xhat, _inv = normed(h1)
        r.n2[rows, :] = (xhat * vec[0:1, :] + vec[2:3, :]).astype(bf16)
        r.acc[rows, :] = h1 + vec[3:4, :]
    row_loop(second_norm)

    def hidden(j, _):
        up = square(r.w, 1, j)
        for c in range(3):
            cols = slice(c * 256, (c + 1) * 256)
            u = nt(r.n2[...], up[cols]) + vec[pl.ds(4 + j, 1), cols]
            cdf = 0.5 * (1.0 + lax.erf(u * 0.7071067811865476))
            r.act[j, :, cols] = (u * cdf).astype(bf16)
            r.gp[j, :, cols] = (cdf + u * (jnp.exp(-0.5 * u * u) * 0.3989422804014327)).astype(bf16)
        return 0
    lax.fori_loop(0, 4, hidden, 0)


def forward_down(r):
    def hidden(j, _):
        r.acc[...] += nn(r.act[j], square(r.w, 2, j))
        return 0
    lax.fori_loop(0, 4, hidden, 0)


def backward_ffn(r, hook=None):
    vec = r.vec
    dvec = r.dvec

    def hidden(j, _):
        down = square(r.w, 2, j)
        for c in range(3):
            cols = slice(c * 256, (c + 1) * 256)
            du = (nt(r.gy[...], down[cols]) * r.gp[j, :, cols].astype(f32)).astype(bf16)
            r.gp[j, :, cols] = du
            dvec[pl.ds(4 + j, 1), cols] = jnp.sum(du.astype(f32), 0, keepdims=True)
        part = nn(r.gp[j], square(r.w, 1, j))

        @pl.when(j == 0)
        def _():
            r.acc[...] = part

        @pl.when(j > 0)
        def _():
            r.acc[...] += part
        if hook is not None:
            hook(j)
        return 0
    lax.fori_loop(0, 4, hidden, 0)

    def norm_two(rows, sums):
        dn = r.acc[rows, :]
        gy = r.gy[rows, :].astype(f32)
        xhat, inv = normed(r.h1[rows, :])
        dh = gy + norm_back(dn, xhat, inv, vec[0:1, :])
        r.h1[rows, :] = dh
        gh = dh.astype(bf16)
        r.gh[rows, :] = gh
        return (sums[0] + fold(dn * xhat), sums[1] + fold(dn), sums[2] + fold(gh.astype(f32)), sums[3] + fold(gy))
    zero = jnp.zeros((8, 768), f32)
    sums = row_loop(norm_two, (zero,) * 4)
    for row, total in zip((0, 2, 1, 3), sums):
        dvec[row:row + 1, :] = jnp.sum(total, 0, keepdims=True)


def grads_down(r):
    def hidden(j, _):
        r.g[2, j] = tn(r.act[j], r.gy[...]).astype(bf16).reshape(4, 4, 48, 768)
        return 0
    lax.fori_loop(0, 4, hidden, 0)


def grads_up(r):
    def hidden(j, _):
        r.g[1, j] = tn(r.gp[j], r.n2[...]).astype(bf16).reshape(4, 4, 48, 768)
        return 0
    lax.fori_loop(0, 4, hidden, 0)


def backward_attention(r, hook=None):
    dvec = r.dvec
    low = lax.broadcasted_iota(jnp.int32, (IMG, 128), 1) < 64
    zero = jnp.zeros((IMG, 128), bf16)

    def head_group(t, _):
        r.dm[...] = nn(r.gh[...], square(r.w, 0, t, 512, 768)).astype(bf16)

        def image(i):
            rows = slice(i * IMG, (i + 1) * IMG)
            tq, tk, tv, t3, t4 = (r.q[t, rows, k * 128:(k + 1) * 128] for k in range(5))
            d4 = r.dm[rows, 0:128]
            d5 = r.dm[rows, 128:256]

            def head(h, d_full, d_masked, v, q, kt):
                p = r.p[(t * 2 + i) * 3 + h]
                pf = p.astype(f32)
                dv = nn(p, d_full)
                dp = nt(v, d_masked)
                ds = (pf * (dp - jnp.sum(dp * pf, 0, keepdims=True))).astype(bf16)
                return nn(kt, ds), nn(ds, q), dv
            tkt = tk.T
            dq0, dk0, dv0 = head(0, d5, jnp.where(low, d5, zero), tv, tq, tkt[0:64])
            dq1, dk1, dv1 = head(1, d5, jnp.where(low, zero, d5), tv, tq, tkt[64:128])
            dq2, dk2, dv2 = head(2, d4, jnp.where(low, zero, d4), t3, t3, t4.T[0:64])
            r.q[t, rows, 0:128] = (jnp.concatenate([dq0, dq1], 0) * 0.125).astype(bf16).T
            r.q[t, rows, 128:256] = (jnp.where(low, dk0, dk1) * 0.125).astype(bf16)
            r.q[t, rows, 256:384] = jnp.where(low, dv0, dv1).astype(bf16)
            dq2 = jnp.concatenate([(dq2 * 0.125).astype(bf16), jnp.zeros((64, IMG), bf16)], 0).T
            r.q[t, rows, 384:512] = jnp.where(low, dq2, dv2.astype(bf16))
            r.q[t, rows, 512:640] = jnp.where(low, dk2 * 0.125, 0.0).astype(bf16)
        image(0)
        image(1)
        dvec[pl.ds(10 + t, 1), 0:640] = jnp.sum(r.q[t].astype(f32), 0, keepdims=True)
        part = nt(r.q[t], square(r.w, 0, t, 0, 640))

        @pl.when(t == 0)
        def _():
            r.acc[...] = part

        @pl.when(t > 0)
        def _():
            r.acc[...] += part
        if hook is not None:
            hook(t)
        return 0
    lax.fori_loop(0, 4, head_group, 0)


def grads_attention(r):
    def head_group(t, _):
        ga = tn(r.n1[...], r.q[t])
        go = tn(r.gh[...], r.mx[t])
        r.g[0, t, :, :, :, 0:512] = ga[:, 0:512].astype(bf16).reshape(4, 4, 48, 512)
        r.g[0, t, :, :, :, 512:640] = (ga[:, 512:640] + go[:, 0:128]).astype(bf16).reshape(4, 4, 48, 128)
        r.g[0, t, :, :, :, 640:768] = go[:, 128:256].astype(bf16).reshape(4, 4, 48, 128)
        return 0
    lax.fori_loop(0, 4, head_group, 0)


def backward_end(r):
    vec = r.vec
    dvec = r.dvec

    def norm_one(rows, sums):
        dn = r.acc[rows, :]
        xhat, inv = normed(r.x[rows, :].astype(f32))
        dx = r.h1[rows, :] + norm_back(dn, xhat, inv, vec[8:9, :])
        r.dx[rows, :] = dx.astype(bf16)
        return (sums[0] + fold(dn * xhat), sums[1] + fold(dn))
    zero = jnp.zeros((8, 768), f32)
    sums = row_loop(norm_one, (zero,) * 2)
    for row, total in zip((8, 9), sums):
        dvec[row:row + 1, :] = jnp.sum(total, 0, keepdims=True)


SLOTS = (3, 4, 4, 4, 48, 768)
BODY_SCRATCH = dict(
    x=pltpu.VMEM((ROWS, 768), bf16), n1=pltpu.VMEM((ROWS, 768), bf16), q=pltpu.VMEM((4, ROWS, 640), bf16),
    p=pltpu.VMEM((24, IMG, IMG), bf16), mx=pltpu.VMEM((4, ROWS, 256), bf16), acc=pltpu.VMEM((ROWS, 768), f32),
    h1=pltpu.VMEM((ROWS, 768), f32), n2=pltpu.VMEM((ROWS, 768), bf16), act=pltpu.VMEM((4, ROWS, 768), bf16),
    gp=pltpu.VMEM((4, ROWS, 768), bf16), gy=pltpu.VMEM((ROWS, 768), bf16), gh=pltpu.VMEM((ROWS, 768), bf16),
    dm=pltpu.VMEM((ROWS, 256), bf16), dx=pltpu.VMEM((ROWS, 768), bf16),
    vec=pltpu.VMEM((16, 768), f32), dvec=pltpu.VMEM((16, 768), f32),
    w=pltpu.VMEM(SLOTS, bf16), g=pltpu.VMEM(SLOTS, bf16),
)


NAMES = list(BODY_SCRATCH)


def layer_kernel(w_hbm, rows_hbm, vec_hbm, end_hbm, grad_hbm, dvec_hbm, *scratch):
    r = types.SimpleNamespace(**dict(zip(NAMES, scratch)))
    rest = scratch[len(NAMES) :]
    landings, out = rest[:5], r.h1
    stages, sum_landings = rest[5:8], rest[8:11]
    ag_send, ag_recv, rs_send, rs_recv, sum_send, sum_recv, link, local, ready = rest[11:]
    coords = place()
    first = lax.axis_index("pipe") == 0
    second = lax.axis_index("pipe") == 1
    own = [
        pltpu.make_async_copy(
            w_hbm.at[kind], r.w.at[(kind, *(coords[name] for name in LAYOUT[kind]))], local.at[kind]
        )
        for kind in range(3)
    ]
    for copy in own:
        copy.start()
    vec_in = pltpu.make_async_copy(vec_hbm, stages[0].at[0], local.at[3])
    vec_in.start()

    to_x = pltpu.make_async_copy(rows_hbm, r.x, local.at[4])
    to_gy = pltpu.make_async_copy(rows_hbm, r.gy, local.at[4])

    @pl.when(first)
    def _():
        to_x.start()

    @pl.when(second)
    def _():
        to_gy.start()

    enter(coords)
    for copy in own:
        copy.wait()
    vec_in.wait()

    gathers = [Gather(r.w, kind, third, coords, ag_send, ag_recv) for kind in range(3) for third in range(3)]
    sums = [AllSum(stages[k], sum_landings[k], coords, sum_send.at[k], sum_recv.at[k]) for k in range(3)]

    def each(movers, *numbers):
        for number in numbers:
            for mover in movers:
                mover.step(number)

    early, late = gathers[:3], gathers[3:]
    sums[0].start(0)
    each(early, 0)
    each(late, 0)
    sums[0].finish(0)
    sums[0].start(1)
    each(early, 1)
    each(late, 1)
    each(early, 2, 3)
    sums[0].finish(1)
    sums[0].start(2)
    each(late, 2, 3)
    each(early, 4)
    sums[0].finish(2)
    each(late, 4)
    each(early, 5)

    @pl.when(second)
    def _():
        each(late, 5)
        pl.semaphore_wait(ready, 1)

    each(early, 6)

    @pl.when(first)
    def _():
        each(late, 5)

    each(late, 6)
    each(early, 7, 8)

    @pl.when(first)
    def _():
        pl.semaphore_signal(ready, inc=1, device_id=sibling(), device_id_type=MESH)
        each(late, 7)

    r.vec[...] = stages[0][3].astype(f32)
    r.dvec[...] = jnp.zeros_like(r.dvec)

    up = pltpu.make_async_remote_copy(
        src_ref=r.dx, dst_ref=r.x, send_sem=link.at[0], recv_sem=link.at[1], device_id=sibling(), device_id_type=MESH
    )
    down = pltpu.make_async_remote_copy(
        src_ref=r.dx, dst_ref=r.gy, send_sem=link.at[2], recv_sem=link.at[3], device_id=sibling(), device_id_type=MESH
    )
    end = pltpu.make_async_copy(r.dx, end_hbm, local.at[5])

    @pl.when(first)
    def _():
        to_x.wait()

    @pl.when(second)
    def _():
        to_gy.wait()
        each(late, 7)
        up.wait_recv()

    forward_attention(r)
    each(gathers[3:6], 8)
    forward_up(r)
    each(gathers[6:], 8)
    forward_down(r)
    r.dx[...] = r.acc[...].astype(bf16)

    @pl.when(first)
    def _():
        up.start()

    @pl.when(second)
    def _():
        end.start()

    for gather in gathers:
        gather.drain()
    sums[0].drain()

    @pl.when(first)
    def _():
        up.wait_send()
        down.wait_recv()

    scatters = [
        Scatter(r.g, kind, third, coords, landings, rs_send, rs_recv, out) for kind in range(3) for third in range(3)
    ]
    sa, su, sd = scatters[:3], scatters[3:6], scatters[6:]
    grads_down(r)
    each(sd, 0)

    def during_ffn(j):
        @pl.when(j == 2)
        def _():
            each(sd, 1)

    backward_ffn(r, during_ffn)
    stages[1][0] = r.dvec[0:8, :]
    sums[1].start(0)
    grads_up(r)
    each(su, 0)

    def during_attention(t):
        @pl.when(t == 1)
        def _():
            each(su, 1)

        @pl.when(t == 3)
        def _():
            sums[1].finish(0)
            sums[1].start(1)
            each(sd, 2, 3)

    backward_attention(r, during_attention)

    @pl.when(second)
    def _():
        end.wait()

    backward_end(r)

    @pl.when(first)
    def _():
        end.start()

    @pl.when(second)
    def _():
        down.start()

    stages[2][0] = r.dvec[8:16, :]
    sums[2].start(0)
    grads_attention(r)
    sums[2].finish(0)
    sums[2].start(1)
    each(sa, 0)
    sums[1].finish(1)
    sums[1].start(2)
    each(sd, 4)
    each(su, 2, 3)
    sums[2].finish(1)
    sums[2].start(2)
    each(sa, 1)
    each(sd, 5, 6)
    each(su, 4)
    sums[1].finish(2)
    each(sa, 2, 3)
    each(sd, 7)
    each(su, 5, 6)
    sums[2].finish(2)
    each(sa, 4)
    each(sd, 8)
    each(su, 7)
    each(sa, 5, 6)
    each(su, 8)
    each(sa, 7, 8)
    copies = [
        pltpu.make_async_copy(out.at[pl.ds(0, 144)], grad_hbm, local.at[0]),
        pltpu.make_async_copy(stages[1].at[3], dvec_hbm.at[pl.ds(0, 8)], local.at[1]),
        pltpu.make_async_copy(stages[2].at[3], dvec_hbm.at[pl.ds(8, 8)], local.at[2]),
    ]
    for copy in copies:
        copy.start()
    for scatter in scatters:
        scatter.drain()
    for some in sums[1:]:
        some.drain()

    @pl.when(first)
    def _():
        end.wait()

    @pl.when(second)
    def _():
        down.wait_send()

    for copy in copies:
        copy.wait()


def units(q, k, v, o):
    order = ((q, 0), (q, 1), (k, 0), (k, 1), (v, 0), (v, 1), (q, 2), (v, 2), (k, 2), (o, 2), (o, 0), (o, 1))
    return jnp.concatenate([a[..., h, :] for a, h in order], -1)


def split_units(joined):
    part = [joined[..., 64 * n : 64 * n + 64] for n in range(joined.shape[-1] // 64)]
    pick = lambda *numbers: jnp.stack([part[n] for n in numbers], -2)
    return pick(0, 1, 6), pick(2, 3, 8), pick(4, 5, 7), (pick(10, 11, 9) if len(part) > 10 else None)


def on_device(
    boundary, loads, norm_gains, row_biases, w_qkv, qv_bias, w_out, w_up, up_bias, w_down
):
    first = lax.axis_index("pipe") == 0
    fsdp, tp = lax.axis_index("fsdp"), lax.axis_index("tp")
    chip = fsdp * 4 + tp
    live = (tp < loads[:, 0])[:, None, None]
    rows = jnp.where(first | live, boundary[0], 0)
    rows = jnp.pad(rows, ((0, 0), (0, IMG - SEQ), (0, 0))).reshape(ROWS, 768)

    wq = w_qkv[0]
    wo = w_out[0].transpose(2, 0, 1)
    weights = jnp.stack([units(wq[:, 0], wq[:, 1], wq[:, 2], wo), w_up[0].T, w_down[0]], 0)

    lanes = jnp.arange(768, dtype=jnp.int32)
    gains, biases = norm_gains[0], row_biases[0]
    small = jnp.concatenate([gains[1:], biases[1:], gains[:1], biases[:1]], 0)
    small = jnp.where(lanes // 12 == chip, jnp.tile(small, (1, 64)), 0)
    hidden = jnp.arange(3072, dtype=jnp.int32)
    hidden = jnp.where(hidden // 48 == chip, jnp.tile(up_bias[0], 64), 0).reshape(4, 768)
    heads = jnp.where(
        jnp.arange(64, dtype=jnp.int32) // 4 == fsdp, jnp.tile(qv_bias[0], (1, 1, 16)), 0
    )
    none = jnp.zeros_like(heads[0])
    heads = units(heads[0], none, heads[1], none)
    heads = jnp.where(jnp.arange(4, dtype=jnp.int32)[:, None] == tp, heads[None], 0)
    vec = jnp.concatenate([small[:4], hidden, small[4:], heads, jnp.zeros((2, 768), bf16)], 0)

    anywhere = pl.BlockSpec(memory_space=pl.ANY)
    dma = pltpu.SemaphoreType.DMA
    end, grads, dvec = pl.pallas_call(
        layer_kernel,
        out_shape=(
            jax.ShapeDtypeStruct((ROWS, 768), bf16),
            jax.ShapeDtypeStruct((144, 768), f32),
            jax.ShapeDtypeStruct((16, 768), f32),
        ),
        in_specs=[anywhere] * 3,
        out_specs=(anywhere,) * 3,
        scratch_shapes=[
            *BODY_SCRATCH.values(),
            *LANDINGS,
            pltpu.VMEM((4, 16, 768), bf16),
            pltpu.VMEM((4, 8, 768), f32),
            pltpu.VMEM((4, 8, 768), f32),
            pltpu.VMEM((3, 3, 16, 768), bf16),
            pltpu.VMEM((3, 3, 8, 768), f32),
            pltpu.VMEM((3, 3, 8, 768), f32),
            dma((9, 3, 4)),
            dma((9, 3, 4)),
            dma((9, 3, 4)),
            dma((9, 3, 4)),
            dma((3, 3, 3)),
            dma((3, 3, 3)),
            dma((4,)),
            dma((6,)),
            pltpu.SemaphoreType.REGULAR,
        ],
        compiler_params=pltpu.CompilerParams(
            collective_id=0, has_side_effects=True, vmem_limit_bytes=63 * 2**20
        ),
    )(weights, rows, vec)

    end = end.reshape(2, IMG, 768)[:, :SEQ]
    ends = jnp.where(first | live, end, 0)[None]
    gq, gk, gv, go = split_units(grads[:48])
    mine = lax.dynamic_slice(dvec, (0, chip * 12), (10, 12))
    up_row = lax.dynamic_slice(dvec[4:8].reshape(3072), (chip * 48,), (48,))
    head_row = lax.dynamic_slice(dvec, (10 + tp, 0), (1, 640))[0]
    hq, _, hv, _ = split_units(head_row)
    head_grads = lax.dynamic_slice(jnp.stack([hq, hv], 0), (0, 0, fsdp * 4), (2, 3, 4))
    return (
        ends,
        jnp.stack([mine[8], mine[0]], 0)[None],
        jnp.stack([mine[9], mine[1], mine[2], mine[3]], 0)[None],
        jnp.stack([gq, gk, gv], 1)[None],
        head_grads[None],
        go.transpose(1, 2, 0)[None],
        grads[48:96].T[None],
        up_row[None],
        grads[96:][None],
    )


def solution(mesh):
    placed = (
        P("pipe", None, ("fsdp", "tp"), None),
        P(None, "fsdp"),
        P("pipe", None, ("fsdp", "tp")),
        P("pipe", None, ("fsdp", "tp")),
        P("pipe", "fsdp", None, "tp", None),
        P("pipe", None, "tp", "fsdp"),
        P("pipe", "tp", None, "fsdp"),
        P("pipe", None, ("fsdp", "tp")),
        P("pipe", ("fsdp", "tp")),
        P("pipe", ("fsdp", "tp"), None),
    )
    return jax.shard_map(
        on_device,
        mesh=mesh,
        in_specs=placed,
        out_specs=(placed[0], *placed[2:]),
        check_vma=False,
    )
```
